128 devices in a mesh: seq: 16 (over z, x), head: 8 (over y, core).
Axes of the slice: x: 4, y: 4, z: 4, core: 2. Of those that a mesh axis runs over, the one named last changes fastest.
Arguments:
- scaled_input: bfloat16 [16384, 16384], P('seq', 'head'), may hold values from -0.059814453 to 0.059814453
- out_grad: bfloat16 [16384, 16384], P('seq', 'head'), may hold values from -1.796875 to 1.796875
- write_proj: bfloat16 [16384, 128], P('seq'), may hold values from -0.5 to 0.5
- read_proj: bfloat16 [16384, 128], P('seq'), may hold values from -0.5 to 0.5
- log_decay: float32 [256, 16384], P('head', 'seq'), may hold values from -0.8 to 0, as said below
Outputs:
- grad_input: bfloat16 [16384, 16384], P('seq', 'head')
- grad_write: bfloat16 [16384, 128], P(('seq', 'head'))
- grad_read: bfloat16 [16384, 128], P(('seq', 'head'))
The draws below stay inside these ranges and needn't reach their ends.
Inputs may be any that keep to these rules, and one draw needn't show every extreme that they name: `log_decay`: logarithms of the per-token decays of each head.
All inputs are finite; a program needn't handle non-finite values.
Results may differ from the reference program's by a relative error of at most 0.0045.
Values sent between devices are 32-bit elements; how exact they have to be, the bound alone decides.
No kernel may reach another device: no remote copies, remote signals or barrier semaphores. Data moves between devices by JAX's collectives and lax.ppermute only.
A program may use at most 192 MiB of HBM per device.

```python
import math
import jax
import jax.numpy as jnp
from jax import lax

HEAD_DIM = 64
STATE = 128
BLOCK = 256
TOK_DEV = 1024
HEADS = 256
INNER = 16384
SEGMENT_TOKENS = 16384


def draw_log_decay(key, part):
    random_subkeys = [jax.random.fold_in(key, 11 + offset) for offset in range(8)]
    quick_share = 8
    quick_heads = jax.random.randint(random_subkeys[0], (HEADS,), 0, 16) < quick_share
    slow_rate = jax.random.uniform(random_subkeys[1], (HEADS,), jnp.float32, 0.1, 0.4) / SEGMENT_TOKENS
    quick_rate = jnp.exp(jax.random.uniform(random_subkeys[2], (HEADS,), jnp.float32, math.log(1.0 / 50.0), math.log(1.0 / 30.0)))
    decay_factors = jnp.where(quick_heads, quick_rate, slow_rate)
    split_multiplier = jnp.exp(jax.random.uniform(random_subkeys[3], (HEADS, SEGMENT_TOKENS // TOK_DEV), jnp.float32, math.log(0.5), math.log(2.0)))
    split_multiplier = jnp.repeat(split_multiplier, TOK_DEV, axis=1, total_repeat_length=SEGMENT_TOKENS)
    jaggedness_level = jax.random.uniform(random_subkeys[4], (HEADS, SEGMENT_TOKENS), jnp.float32, 0.5, 1.5)
    leading_spike = jax.random.randint(random_subkeys[5], (), 0, SEGMENT_TOKENS)
    trailing_spike = (leading_spike + jax.random.randint(random_subkeys[6], (), 1, SEGMENT_TOKENS)) % SEGMENT_TOKENS
    spike_values = jnp.stack([leading_spike, trailing_spike])
    loss_values = jax.random.uniform(random_subkeys[7], (2,), jnp.float32, 0.2, 0.5)
    token_positions = jnp.arange(SEGMENT_TOKENS)
    spike_logarithm = jnp.sum(jnp.where(token_positions[None, :] == spike_values[:, None], jnp.log(1.0 - loss_values)[:, None], 0.0), axis=0)
    return -decay_factors[:, None] * split_multiplier * jaggedness_level + spike_logarithm[None, :]


def strengthened(drawn, own_key, source, target, parts, factor):
    owner, partner = [(jnp.arange(drawn.shape[position]) // (drawn.shape[position] // parts)).reshape([-1 if axis == position else 1 for axis in range(drawn.ndim)]) for position in (source, target)]
    chosen = jax.random.permutation(own_key, parts)[partner]
    strong = (owner == chosen) | (owner == (partner + parts // 2) % parts)
    return jnp.where(strong, factor * drawn, drawn)


def block_scale(key, dims, cuts, least, largest):
    loudness = 1.0
    for position, shards_of in cuts:
        steps = jax.random.uniform(jax.random.fold_in(jax.random.fold_in(key, 6), position), (shards_of,), jnp.float32, least / len(cuts), largest / len(cuts))
        loudness = loudness * jnp.repeat(jnp.exp(steps), dims[position] // shards_of).reshape((-1,) + (1,) * (len(dims) - 1 - position))
    return loudness


def scatter_about(key, extent, width, limit, shards=(), dtype=jnp.bfloat16):
    entries = width * jax.random.normal(key, extent, jnp.float32)
    if shards:
        entries = entries * block_scale(key, extent, shards, -0.22, 0.18)
    return jnp.clip(entries, -limit, limit).astype(dtype)


def bell_draw_with(key, shape, scale, most, cuts, heavy, kind=jnp.bfloat16):
    result = scale * jax.random.normal(key, shape, jnp.float32)
    if cuts:
        result = result * block_scale(key, shape, cuts, -0.22, 0.18)
    return jnp.clip(strengthened(result, jax.random.fold_in(key, 3), *heavy), -most, most).astype(kind)


def setup_inputs(seed: int = 0) -> dict:
    key_list = jax.random.split(jax.random.key(seed), 6)
    return {
        "scaled_input": scatter_about(key_list[0], (SEGMENT_TOKENS, INNER), 0.01, 0.059814453, ((0, 16), (1, 8))),
        "out_grad": bell_draw_with(key_list[1], (SEGMENT_TOKENS, INNER), 0.3, 1.796875, ((0, 16), (1, 8)), (1, 0, 16, 2.0)),
        "write_proj": scatter_about(key_list[2], (SEGMENT_TOKENS, STATE), STATE ** -0.5, 0.5, ((0, 16),)),
        "read_proj": scatter_about(key_list[3], (SEGMENT_TOKENS, STATE), STATE ** -0.5, 0.5, ((0, 16),)),
        "log_decay": draw_log_decay(jax.random.fold_in(key_list[5], 71), 0),
    }


highest = lax.Precision.HIGHEST


def block_terms(inputs, grads, writes, reads, cumulative, entering, leaving):
    length = cumulative.shape[1]
    token_positions = jnp.arange(length)
    upper = token_positions[None, :] >= token_positions[:, None]
    spread = cumulative[:, None, :] - cumulative[:, :, None]
    decay_mat = jnp.exp(jnp.where(upper[None], spread, -jnp.inf))
    inputs_f = inputs.astype(jnp.float32)
    grads_f = grads.astype(jnp.float32)
    writes_f = writes.astype(jnp.float32)
    reads_f = reads.astype(jnp.float32)
    to_end = jnp.exp(cumulative[:, -1:] - cumulative)
    from_start = jnp.exp(cumulative)
    pairs = jnp.dot(writes, reads.T, preferred_element_type=jnp.float32)
    weights_x = (decay_mat * pairs[None]).astype(jnp.bfloat16)
    weights_x = lax.optimization_barrier(weights_x).astype(jnp.float32)
    intra = jnp.einsum('hij,jhp->ihp', weights_x, grads_f, precision=highest)
    inter = to_end.T[:, :, None] * jnp.einsum('in,hnp->ihp', writes_f, leaving, precision=highest)
    grad_input = (intra + inter).astype(jnp.bfloat16).reshape(length, -1)
    cross = jnp.einsum('ihp,jhp->hij', inputs_f, grads_f, precision=highest)
    weights_w = (decay_mat * cross).astype(jnp.bfloat16)
    weights_w = lax.optimization_barrier(weights_w).astype(jnp.float32)
    scaled_in = to_end.T[:, :, None] * inputs_f
    scaled_grad = from_start.T[:, :, None] * grads_f
    part_write = jnp.einsum('hij,jn->in', weights_w, reads_f, precision=highest) + jnp.einsum('ihp,hnp->in', scaled_in, leaving, precision=highest)
    part_read = jnp.einsum('hij,in->jn', weights_w, writes_f, precision=highest) + jnp.einsum('jhp,hnp->jn', scaled_grad, entering, precision=highest)
    return grad_input, part_write, part_read


def reference(scaled_input, out_grad, write_proj, read_proj, log_decay):
    count = SEGMENT_TOKENS // BLOCK
    inputs = scaled_input.reshape(count, BLOCK, HEADS, HEAD_DIM)
    grads = out_grad.reshape(count, BLOCK, HEADS, HEAD_DIM)
    writes = write_proj.reshape(count, BLOCK, STATE)
    reads = read_proj.reshape(count, BLOCK, STATE)
    cumulative = jnp.cumsum(log_decay.reshape(HEADS, count, BLOCK), axis=2).transpose(1, 0, 2)

    def forward(carried, pieces):
        block_in, block_write, block_cum = pieces
        to_end = jnp.exp(block_cum[:, -1:] - block_cum)
        scaled = to_end.T[:, :, None] * block_in.astype(jnp.float32)
        local = jnp.einsum('in,ihp->hnp', block_write.astype(jnp.float32), scaled, precision=highest)
        return jnp.exp(block_cum[:, -1])[:, None, None] * carried + local, carried

    def backward(carried, pieces):
        block_grad, block_read, block_cum = pieces
        scaled = jnp.exp(block_cum).T[:, :, None] * block_grad.astype(jnp.float32)
        local = jnp.einsum('in,ihp->hnp', block_read.astype(jnp.float32), scaled, precision=highest)
        return jnp.exp(block_cum[:, -1])[:, None, None] * carried + local, carried

    start = jnp.zeros((HEADS, STATE, HEAD_DIM), jnp.float32)
    entering = lax.scan(forward, start, (inputs, writes, cumulative))[1]
    leaving = lax.scan(backward, start, (grads, reads, cumulative), reverse=True)[1]
    results = lax.map(lambda pieces: block_terms(*pieces), (inputs, grads, writes, reads, cumulative, entering, leaving))
    grad_input = results[0].reshape(SEGMENT_TOKENS, INNER)
    grad_write = results[1].reshape(SEGMENT_TOKENS, STATE).astype(jnp.bfloat16)
    grad_read = results[2].reshape(SEGMENT_TOKENS, STATE).astype(jnp.bfloat16)
    return (grad_input, grad_write, grad_read)
```

```python
import jax
import jax.numpy as jnp
from jax import lax
from jax.experimental import pallas as pl
from jax.experimental.pallas import tpu as pltpu
from jax.sharding import PartitionSpec as P

SUB = 128
LANES = 128
WIDE = 256
MIDDLE = SUB // 2 - 1
F32 = jnp.float32
BF16 = jnp.bfloat16


def dot(a, b, dims=((1,), (0,)), precision=None):
    return lax.dot_general(a, b, (dims, ((), ())), precision=precision, preferred_element_type=F32)


def running_sum(decays, start):
    rows = lax.broadcasted_iota(jnp.int32, (SUB, SUB), 0)
    columns = lax.broadcasted_iota(jnp.int32, (SUB, SUB), 1)
    lower = jnp.where(rows >= columns, 1.0, 0.0).astype(F32)
    return dot(lower, decays[:, start : start + SUB], ((1,), (1,)), lax.Precision.HIGHEST)


def two_terms(values, heads):
    lane = lax.broadcasted_iota(jnp.int32, values.shape, 1)
    high = values.astype(BF16).astype(F32)
    kept = jnp.where(lane < heads, high, jnp.where(lane < 2 * heads, values - high, 0.0))
    return kept.astype(BF16)


def spread_matrix(heads, head_size, first_head):
    row = lax.broadcasted_iota(jnp.int32, (LANES, WIDE), 0)
    column = lax.broadcasted_iota(jnp.int32, (LANES, WIDE), 1)
    same = lax.rem(row, heads) == first_head + column // head_size
    return jnp.where(same, 1.0, 0.0).astype(BF16)


def repeated(decays):
    return jnp.concatenate([decays] * (LANES // decays.shape[0]), axis=0)


def summary_kernel(x_ref, g_ref, w_ref, r_ref, ld_ref, out_ref, sums, fx, fg, total, wt, rt):
    heads, tokens = ld_ref.shape
    head_size = x_ref.shape[1] * pl.num_programs(0) // heads
    step = pl.program_id(0)

    @pl.when(step == 0)
    def _():
        decays = repeated(ld_ref[...])
        offset = jnp.zeros((1, LANES), F32)
        for start in range(0, tokens, SUB):
            part = running_sum(decays, start) + offset
            sums[start : start + SUB] = part
            offset = part[SUB - 1 :]
            wt[:, start : start + SUB] = w_ref[start : start + SUB].T
            rt[:, start : start + SUB] = r_ref[start : start + SUB].T
        total[...] = two_terms(jnp.broadcast_to(jnp.exp(offset), (16, LANES)), heads)
        for start in range(0, tokens, SUB):
            part = sums[start : start + SUB]
            fx[start : start + SUB] = two_terms(jnp.exp(offset - part), heads)
            fg[start : start + SUB] = two_terms(jnp.exp(part), heads)

    spread = spread_matrix(heads, head_size, step * (WIDE // head_size))
    scaled_x = (x_ref[...].astype(F32) * dot(fx[...], spread)).astype(BF16)
    scaled_g = (g_ref[...].astype(F32) * dot(fg[...], spread)).astype(BF16)
    written = dot(wt[...], scaled_x)
    collected = dot(rt[...], scaled_g)
    decay = dot(total[...], spread)[:8]
    state = written.shape[0]
    for pair in range(WIDE // LANES):
        lanes = slice(pair * LANES, (pair + 1) * LANES)
        out_ref[pair, :state] = written[:, lanes]
        out_ref[pair, state : 2 * state] = collected[:, lanes]
        out_ref[pair, 2 * state :] = decay[:, lanes]


def scan_kernel(in_ref, out_ref):
    shards = in_ref.shape[0]
    state = out_ref.shape[1] // 2
    carried = jnp.zeros((state, LANES), F32)
    for shard in range(shards):
        out_ref[shard, :state] = carried
        carried = in_ref[shard, 2 * state : 2 * state + 1] * carried + in_ref[shard, :state]
    carried = jnp.zeros((state, LANES), F32)
    for shard in reversed(range(shards)):
        out_ref[shard, state:] = carried
        carried = in_ref[shard, 2 * state : 2 * state + 1] * carried + in_ref[shard, state : 2 * state]


def grads_kernel(
    x_ref, g_ref, st_ref, w_ref, r_ref, ld_ref, gi_ref, out_ref, fa, fb, fuv, pw, wt, rt, acc, scale, right
):
    heads, tokens = ld_ref.shape
    head_size = x_ref.shape[1] * pl.num_programs(0) // heads
    state = w_ref.shape[1]
    count = tokens // SUB
    step = pl.program_id(0)
    rows = lax.broadcasted_iota(jnp.int32, (SUB, SUB), 0)
    columns = lax.broadcasted_iota(jnp.int32, (SUB, SUB), 1)
    upper = columns >= rows

    @pl.when(step == 0)
    def _():
        decays = repeated(ld_ref[...])
        middles = []
        afters = []
        for k in range(count):
            tok = slice(k * SUB, (k + 1) * SUB)
            part = running_sum(decays, k * SUB)
            middle = part[MIDDLE : MIDDLE + 1]
            fa[tok] = two_terms(jnp.exp(middle - part), heads)
            fb[tok] = two_terms(jnp.exp(part - middle), heads)
            middles.append(middle)
            afters.append(part[SUB - 1 :] - middle)
            write, read = w_ref[tok], r_ref[tok]
            pairs = jnp.where(upper, dot(write, read, ((1,), (1,))), 0.0).astype(BF16)
            pw[k] = jnp.concatenate([pairs, write], axis=1)
            wt[k] = write.T
            rt[k] = read.T
        into = [middles[0]] + [middles[k] + afters[k - 1] for k in range(1, count)]
        back = [afters[k] + middles[k + 1] for k in range(count - 1)] + [afters[count - 1]]
        fuv[...] = two_terms(jnp.exp(jnp.concatenate(into + back, axis=0)), heads)
        acc[...] = jnp.zeros_like(acc)

    spread = spread_matrix(heads, head_size, step * (WIDE // head_size))
    factor = dot(fuv[...], spread)
    entering = jnp.concatenate([st_ref[p, :state] for p in range(WIDE // LANES)], axis=1)
    leaving = jnp.concatenate([st_ref[p, state:] for p in range(WIDE // LANES)], axis=1)

    back = factor[2 * count - 1 : 2 * count] * leaving
    for k in reversed(range(count)):
        tok = slice(k * SUB, (k + 1) * SUB)
        scaled_g = (g_ref[tok].astype(F32) * dot(fb[tok], spread)).astype(BF16)
        stacked = jnp.concatenate([scaled_g, back.astype(BF16)], axis=0)
        right[k] = stacked
        factors = dot(fa[tok], spread)
        scale[tok] = factors
        gi_ref[tok] = (factors * dot(pw[k], stacked)).astype(BF16)
        if k:
            back = factor[count + k - 1 : count + k] * (back + dot(rt[k], scaled_g))

    into = factor[:1] * entering
    for k in range(count):
        tok = slice(k * SUB, (k + 1) * SUB)
        scaled_x = (x_ref[tok].astype(F32) * scale[tok]).astype(BF16)
        stacked = jnp.concatenate([scaled_x, into.astype(BF16)], axis=0)
        acc[k] += dot(stacked, right[k], ((1,), (1,)))
        if k + 1 < count:
            into = factor[k + 1 : k + 2] * (into + dot(wt[k], scaled_x))

    @pl.when(step == pl.num_programs(0) - 1)
    def _():
        for k in range(count):
            tok = slice(k * SUB, (k + 1) * SUB)
            weights = jnp.where(upper, acc[k, :SUB, :SUB], 0.0).astype(BF16)
            out_ref[k, :, :state] = dot(weights, r_ref[tok]) + acc[k, :SUB, SUB:]
            out_ref[k, :, state:] = (dot(wt[k], weights) + acc[k, SUB:, :SUB]).T


def body(scaled_input, out_grad, write_proj, read_proj, log_decay):
    tokens, width = scaled_input.shape
    heads = log_decay.shape[0]
    state = write_proj.shape[1]
    shards = lax.axis_size("seq")
    count = tokens // SUB
    steps = width // WIDE
    pairs = WIDE // LANES
    wide = pl.BlockSpec((tokens, WIDE), lambda i: (0, i))
    whole = pl.BlockSpec((tokens, state), lambda i: (0, 0))
    decays = pl.BlockSpec((heads, tokens), lambda i: (0, 0))
    params = pltpu.CompilerParams(vmem_limit_bytes=48 * 2**20, dimension_semantics=("arbitrary",))

    summary = pl.pallas_call(
        summary_kernel,
        grid=(steps,),
        in_specs=[wide, wide, whole, whole, decays],
        out_specs=pl.BlockSpec((pairs, 2 * state + 8, LANES), lambda i: (i, 0, 0)),
        out_shape=jax.ShapeDtypeStruct((width // LANES, 2 * state + 8, LANES), F32),
        scratch_shapes=[
            pltpu.VMEM((tokens, LANES), F32),
            pltpu.VMEM((tokens, LANES), BF16),
            pltpu.VMEM((tokens, LANES), BF16),
            pltpu.VMEM((16, LANES), BF16),
            pltpu.VMEM((state, tokens), BF16),
            pltpu.VMEM((state, tokens), BF16),
        ],
        compiler_params=params,
        name="summary",
    )(scaled_input, out_grad, write_proj, read_proj, log_decay)

    every = lax.all_to_all(summary, "seq", 0, 0, tiled=True)
    states = pl.pallas_call(
        scan_kernel,
        out_shape=jax.ShapeDtypeStruct((shards, 2 * state, LANES), F32),
        compiler_params=pltpu.CompilerParams(vmem_limit_bytes=48 * 2**20),
        name="scan",
    )(every)
    own = lax.all_to_all(states, "seq", 0, 0, tiled=True)

    grad_input, parts = pl.pallas_call(
        grads_kernel,
        grid=(steps,),
        in_specs=[
            wide,
            wide,
            pl.BlockSpec((pairs, 2 * state, LANES), lambda i: (i, 0, 0)),
            whole,
            whole,
            decays,
        ],
        out_specs=[wide, pl.BlockSpec((count, SUB, 2 * state), lambda i: (0, 0, 0))],
        out_shape=[
            jax.ShapeDtypeStruct((tokens, width), BF16),
            jax.ShapeDtypeStruct((count, SUB, 2 * state), F32),
        ],
        scratch_shapes=[
            pltpu.VMEM((tokens, LANES), BF16),
            pltpu.VMEM((tokens, LANES), BF16),
            pltpu.VMEM((2 * count, LANES), BF16),
            pltpu.VMEM((count, SUB, SUB + state), BF16),
            pltpu.VMEM((count, state, SUB), BF16),
            pltpu.VMEM((count, state, SUB), BF16),
            pltpu.VMEM((count, SUB + state, SUB + state), F32),
            pltpu.VMEM((tokens, WIDE), F32),
            pltpu.VMEM((count, SUB + state, WIDE), BF16),
        ],
        compiler_params=params,
        name="grads",
    )(scaled_input, out_grad, own, write_proj, read_proj, log_decay)

    shared = lax.all_to_all(parts, "head", 0, 0, tiled=True).sum(axis=0)
    return grad_input, shared[:, :state].astype(BF16), shared[:, state:].astype(BF16)


def solution(mesh):
    return jax.shard_map(
        body,
        mesh=mesh,
        in_specs=(
            P("seq", "head"),
            P("seq", "head"),
            P("seq", None),
            P("seq", None),
            P("head", "seq"),
        ),
        out_specs=(P("seq", "head"), P(("seq", "head"), None), P(("seq", "head"), None)),
        check_vma=False,
    )
```

```python
import jax
import jax.numpy as jnp
from jax import lax
from jax.experimental import pallas as pl
from jax.experimental.pallas import tpu as pltpu
from jax.sharding import PartitionSpec as P

SUB = 128
LANES = 128
WIDE = 512
WIDE2 = 1024
MIDDLE = SUB // 2 - 1
F32 = jnp.float32
BF16 = jnp.bfloat16


def dot(a, b, dims=((1,), (0,))):
    return lax.dot_general(a, b, (dims, ((), ())), preferred_element_type=F32)


def running_sums(decays):
    rows = lax.broadcasted_iota(jnp.int32, (SUB, SUB), 0)
    columns = lax.broadcasted_iota(jnp.int32, (SUB, SUB), 1)
    lower = jnp.where(rows >= columns, 1.0, 0.0).astype(BF16)
    first = decays.astype(BF16)
    left = decays - first.astype(F32)
    second = left.astype(BF16)
    third = (left - second.astype(F32)).astype(BF16)
    sums = []
    for start in range(0, decays.shape[1], SUB):
        tok = slice(start, start + SUB)
        a, b, c = (dot(lower, term[:, tok], ((1,), (1,))) for term in (first, second, third))
        sums.append(a + (b + c))
    return sums


def two_terms(values, heads):
    lane = lax.broadcasted_iota(jnp.int32, values.shape, 1)
    high = values.astype(BF16).astype(F32)
    kept = jnp.where(lane < heads, high, jnp.where(lane < 2 * heads, values - high, 0.0))
    return kept.astype(BF16)


def spread_matrix(heads, head_size, wide, step):
    row = lax.broadcasted_iota(jnp.int32, (LANES, wide), 0)
    column = lax.broadcasted_iota(jnp.int32, (LANES, wide), 1)
    same = lax.rem(row, heads) == (step * wide + column) // head_size
    return jnp.where(same, 1.0, 0.0).astype(BF16)


def summary_kernel(
    x_hbm, g_hbm, w_hbm, r_hbm, ld_hbm, out_ref, xs_ref, gs_ref, fa, between, pw, wt, rt, fb, ends, xb, gb, w_ref, r_ref, ld_ref, sems
):
    heads, tokens = ld_ref.shape
    width = xs_ref.shape[1]
    head_size = width // heads
    state = w_ref.shape[1]
    count = tokens // SUB
    steps = width // WIDE

    small = [
        pltpu.make_async_copy(source, target, sems.at[2 * steps + n])
        for n, (source, target) in enumerate(((ld_hbm, ld_ref), (w_hbm, w_ref), (r_hbm, r_ref)))
    ]
    for copy in small:
        copy.start()

    def load(source, target, step, sem):
        columns = pl.ds(pl.multiple_of(step * WIDE, WIDE), WIDE)
        return pltpu.make_async_copy(source.at[:, columns], target.at[step], sems.at[sem])

    for step in range(steps):
        load(x_hbm, xb, step, step).start()
        load(g_hbm, gb, step, steps + step).start()
    for copy in small:
        copy.wait()

    decays = jnp.concatenate([ld_ref[...]] * (LANES // heads), axis=0)
    sums = running_sums(decays)
    rows = lax.broadcasted_iota(jnp.int32, (SUB, SUB), 0)
    columns = lax.broadcasted_iota(jnp.int32, (SUB, SUB), 1)
    before = jnp.zeros((1, LANES), F32)
    upto = []
    middles = []
    afters = []
    for k in range(count):
        tok = slice(k * SUB, (k + 1) * SUB)
        middle, end = sums[k][MIDDLE : MIDDLE + 1], sums[k][SUB - 1 :]
        fa[tok] = two_terms(jnp.exp(middle - sums[k]), heads)
        fb[tok] = two_terms(jnp.exp(sums[k] - middle), heads)
        upto.append(before + middle)
        before = before + end
        middles.append(middle)
        afters.append(end - middle)
        write, read = w_ref[tok], r_ref[tok]
        pairs = jnp.where(columns >= rows, dot(write, read, ((1,), (1,))), 0.0).astype(BF16)
        pw[k] = jnp.concatenate([pairs, write], axis=1)
        wt[k] = write.T
        rt[k] = read.T
    into = [middles[0]] + [middles[k] + afters[k - 1] for k in range(1, count)]
    back = [afters[k] + middles[k + 1] for k in range(count - 1)] + [afters[count - 1]]
    between[...] = two_terms(jnp.exp(jnp.concatenate(into + back, axis=0)), heads)
    to_end = [before - part for part in upto]
    whole = [before] * 16
    ends[...] = two_terms(jnp.exp(jnp.concatenate(to_end + upto + whole, axis=0)), heads)

    @pl.loop(0, steps)
    def _(step):
        load(x_hbm, xb, step, step).wait()
        load(g_hbm, gb, step, steps + step).wait()
        lanes = pl.ds(pl.multiple_of(step * WIDE, WIDE), WIDE)
        spread = spread_matrix(heads, head_size, WIDE, step)
        factor = dot(ends[...], spread)
        written = jnp.zeros((state, WIDE), F32)
        collected = jnp.zeros((state, WIDE), F32)
        xs_ref[:, lanes] = (xb[step].astype(F32) * dot(fa[...], spread)).astype(BF16)
        gs_ref[:, lanes] = (gb[step].astype(F32) * dot(fb[...], spread)).astype(BF16)
        for k in range(count):
            tok = slice(k * SUB, (k + 1) * SUB)
            written += factor[k : k + 1] * dot(wt[k], xs_ref[tok, lanes])
            collected += factor[count + k : count + k + 1] * dot(rt[k], gs_ref[tok, lanes])
        for pair in range(WIDE // LANES):
            part = slice(pair * LANES, (pair + 1) * LANES)
            to = step * (WIDE // LANES) + pair
            out_ref[to, :state] = written[:, part]
            out_ref[to, state : 2 * state] = collected[:, part]
            out_ref[to, 2 * state :] = factor[2 * count : 2 * count + 8, part]


def scan_kernel(in_ref, out_ref):
    shards = in_ref.shape[0]
    state = out_ref.shape[1] // 2
    carried = jnp.zeros((state, LANES), F32)
    for shard in range(shards):
        out_ref[shard, :state] = carried
        carried = in_ref[shard, 2 * state : 2 * state + 1] * carried + in_ref[shard, :state]
    carried = jnp.zeros((state, LANES), F32)
    for shard in reversed(range(shards)):
        out_ref[shard, state:] = carried
        carried = in_ref[shard, 2 * state : 2 * state + 1] * carried + in_ref[shard, state : 2 * state]


def grads_kernel(
    xs_ref, gs_ref, st_ref, r_ref, fa, between, pw, wt, rt, gi_hbm, out_ref, acc, wrote, took, into_s, back_s, gi, sems, *, heads
):
    width = xs_ref.shape[1]
    head_size = width // heads
    count, state, _ = wt.shape
    steps = width // WIDE2
    acc[...] = jnp.zeros_like(acc)

    def store(step):
        lanes = pl.ds(pl.multiple_of(step * WIDE2, WIDE2), WIDE2)
        return pltpu.make_async_copy(gi.at[step], gi_hbm.at[:, lanes], sems.at[step])

    @pl.loop(0, steps)
    def _(step):
        lanes = pl.ds(pl.multiple_of(step * WIDE2, WIDE2), WIDE2)
        first = step * (WIDE2 // LANES)
        spread = spread_matrix(heads, head_size, WIDE2, step)
        factor = dot(between[...], spread)
        for k in range(count):
            tok = slice(k * SUB, (k + 1) * SUB)
            took[k] = dot(rt[k], gs_ref[tok, lanes])
            wrote[k] = dot(wt[k], xs_ref[tok, lanes])

        entering = jnp.concatenate([st_ref[first + p, :state] for p in range(WIDE2 // LANES)], axis=1)
        leaving = jnp.concatenate([st_ref[first + p, state:] for p in range(WIDE2 // LANES)], axis=1)
        back = factor[2 * count - 1 : 2 * count] * leaving
        for k in reversed(range(count)):
            back_s[k] = back.astype(BF16)
            if k:
                back = factor[count + k - 1 : count + k] * (back + took[k])
        into = factor[:1] * entering
        for k in range(count):
            into_s[k] = into.astype(BF16)
            if k + 1 < count:
                into = factor[k + 1 : k + 2] * (into + wrote[k])

        for k in range(count):
            tok = slice(k * SUB, (k + 1) * SUB)
            right = jnp.concatenate([gs_ref[tok, lanes], back_s[k]], axis=0)
            left = jnp.concatenate([xs_ref[tok, lanes], into_s[k]], axis=0)
            gi[step, tok] = (dot(fa[tok], spread) * dot(pw[k], right)).astype(BF16)
            acc[k] += dot(left, right, ((1,), (1,)))
        store(step).start()

    rows = lax.broadcasted_iota(jnp.int32, (SUB, SUB), 0)
    columns = lax.broadcasted_iota(jnp.int32, (SUB, SUB), 1)
    for k in range(count):
        tok = slice(k * SUB, (k + 1) * SUB)
        weights = jnp.where(columns >= rows, acc[k, :SUB, :SUB], 0.0).astype(BF16)
        out_ref[k, :, :state] = dot(weights, r_ref[tok]) + acc[k, :SUB, SUB:]
        out_ref[k, :, state:] = (dot(wt[k], weights) + acc[k, SUB:, :SUB]).T
    for step in range(steps):
        store(step).wait()


PARAMS = pltpu.CompilerParams(vmem_limit_bytes=32 * 2**20)
HERE = pl.BlockSpec(memory_space=pltpu.VMEM)
THERE = pl.BlockSpec(memory_space=pltpu.HBM)


def summarise(x, g, w, r, ld):
    tokens, width = x.shape
    state = w.shape[1]
    count = tokens // SUB
    steps = width // WIDE
    return pl.pallas_call(
        summary_kernel,
        in_specs=[THERE] * 5,
        out_specs=[HERE] * 8,
        out_shape=[
            jax.ShapeDtypeStruct((width // LANES, 2 * state + 8, LANES), F32),
            jax.ShapeDtypeStruct((tokens, width), BF16),
            jax.ShapeDtypeStruct((tokens, width), BF16),
            jax.ShapeDtypeStruct((tokens, LANES), BF16),
            jax.ShapeDtypeStruct((2 * count, LANES), BF16),
            jax.ShapeDtypeStruct((count, SUB, SUB + state), BF16),
            jax.ShapeDtypeStruct((count, state, SUB), BF16),
            jax.ShapeDtypeStruct((count, state, SUB), BF16),
        ],
        scratch_shapes=[
            pltpu.VMEM((tokens, LANES), BF16),
            pltpu.VMEM((2 * count + 16, LANES), BF16),
            pltpu.VMEM((steps, tokens, WIDE), BF16),
            pltpu.VMEM((steps, tokens, WIDE), BF16),
            pltpu.VMEM((tokens, state), BF16),
            pltpu.VMEM((tokens, state), BF16),
            pltpu.VMEM(ld.shape, F32),
            pltpu.SemaphoreType.DMA((2 * steps + 3,)),
        ],
        compiler_params=pltpu.CompilerParams(vmem_limit_bytes=50 * 2**20),
        name="summary",
    )(x, g, w, r, ld)


def scan_shards(every):
    return pl.pallas_call(
        scan_kernel,
        in_specs=[HERE],
        out_specs=HERE,
        out_shape=jax.ShapeDtypeStruct((every.shape[0], every.shape[1] - 8, LANES), F32),
        compiler_params=PARAMS,
        name="scan",
    )(every)


def gradients(scaled_x, scaled_g, own, r, kept, heads):
    tokens, width = scaled_x.shape
    state = r.shape[1]
    count = tokens // SUB
    steps = width // WIDE2

    def kernel(*refs):
        grads_kernel(*refs, heads=heads)

    return pl.pallas_call(
        kernel,
        in_specs=[HERE] * (4 + len(kept)),
        out_specs=[THERE, HERE],
        out_shape=[
            jax.ShapeDtypeStruct((tokens, width), BF16),
            jax.ShapeDtypeStruct((count, SUB, 2 * state), F32),
        ],
        scratch_shapes=[
            pltpu.VMEM((count, SUB + state, SUB + state), F32),
            pltpu.VMEM((count, state, WIDE2), F32),
            pltpu.VMEM((count, state, WIDE2), F32),
            pltpu.VMEM((count, state, WIDE2), BF16),
            pltpu.VMEM((count, state, WIDE2), BF16),
            pltpu.VMEM((steps, tokens, WIDE2), BF16),
            pltpu.SemaphoreType.DMA((steps,)),
        ],
        compiler_params=pltpu.CompilerParams(vmem_limit_bytes=36 * 2**20),
        name="grads",
    )(scaled_x, scaled_g, own, r, *kept)


def body(scaled_input, out_grad, write_proj, read_proj, log_decay):
    heads = log_decay.shape[0]
    state = write_proj.shape[1]
    summary, scaled_x, scaled_g, *kept = summarise(scaled_input, out_grad, write_proj, read_proj, log_decay)
    every = lax.all_to_all(summary, "seq", 0, 0, tiled=True)
    own = lax.all_to_all(scan_shards(every), "seq", 0, 0, tiled=True)
    grad_input, parts = gradients(scaled_x, scaled_g, own, read_proj, kept, heads)
    shared = lax.all_to_all(parts, "head", 0, 0, tiled=True).sum(axis=0)
    return grad_input, shared[:, :state].astype(BF16), shared[:, state:].astype(BF16)


def solution(mesh):
    return jax.shard_map(
        body,
        mesh=mesh,
        in_specs=(
            P("seq", "head"),
            P("seq", "head"),
            P("seq", None),
            P("seq", None),
            P("head", "seq"),
        ),
        out_specs=(P("seq", "head"), P(("seq", "head"), None), P(("seq", "head"), None)),
        check_vma=False,
    )
```

```python
import jax
import jax.numpy as jnp
from jax import lax
from jax.experimental import pallas as pl
from jax.experimental.pallas import tpu as pltpu
from jax.sharding import PartitionSpec as P

SUB = 128
LANES = 128
WIDE = 512
MIDDLE = SUB // 2 - 1
F32 = jnp.float32
BF16 = jnp.bfloat16


def dot(a, b, dims=((1,), (0,))):
    return lax.dot_general(a, b, (dims, ((), ())), preferred_element_type=F32)


def running_sums(decays):
    rows = lax.broadcasted_iota(jnp.int32, (SUB, SUB), 0)
    columns = lax.broadcasted_iota(jnp.int32, (SUB, SUB), 1)
    lower = jnp.where(rows >= columns, 1.0, 0.0).astype(BF16)
    first = decays.astype(BF16)
    left = decays - first.astype(F32)
    second = left.astype(BF16)
    third = (left - second.astype(F32)).astype(BF16)
    sums = []
    for start in range(0, decays.shape[1], SUB):
        tok = slice(start, start + SUB)
        a, b, c = (dot(lower, term[:, tok], ((1,), (1,))) for term in (first, second, third))
        sums.append(a + (b + c))
    return sums


def two_terms(values, heads):
    lane = lax.broadcasted_iota(jnp.int32, values.shape, 1)
    high = values.astype(BF16).astype(F32)
    kept = jnp.where(lane < heads, high, jnp.where(lane < 2 * heads, values - high, 0.0))
    return kept.astype(BF16)


def spread_matrix(heads, head_size, wide, step):
    row = lax.broadcasted_iota(jnp.int32, (LANES, wide), 0)
    column = lax.broadcasted_iota(jnp.int32, (LANES, wide), 1)
    same = lax.rem(row, heads) == (step * wide + column) // head_size
    return jnp.where(same, 1.0, 0.0).astype(BF16)


def summary_kernel(x_ref, g_ref, w_ref, r_ref, ld_ref, out_ref, x1_ref, g1_ref, fx, fg, ends, wt, rt):
    heads, tokens = ld_ref.shape
    wide = x_ref.shape[1]
    head_size = wide * pl.num_programs(0) // heads
    state = w_ref.shape[1]
    step = pl.program_id(0)

    @pl.when(step == 0)
    def _():
        sums = running_sums(jnp.concatenate([ld_ref[...]] * (LANES // heads), axis=0))
        before = jnp.zeros((1, LANES), F32)
        for k in range(len(sums)):
            sums[k] = sums[k] + before
            before = sums[k][SUB - 1 :]
        for k in range(len(sums)):
            tok = slice(k * SUB, (k + 1) * SUB)
            fx[tok] = two_terms(jnp.exp(before - sums[k]), heads)
            fg[tok] = two_terms(jnp.exp(sums[k]), heads)
            wt[:, tok] = w_ref[tok].T
            rt[:, tok] = r_ref[tok].T
        ends[...] = two_terms(jnp.exp(jnp.broadcast_to(before, ends.shape)), heads)

    spread = spread_matrix(heads, head_size, wide, step)
    x1_ref[...] = (x_ref[...].astype(F32) * dot(fx[...], spread)).astype(BF16)
    g1_ref[...] = (g_ref[...].astype(F32) * dot(fg[...], spread)).astype(BF16)
    written = dot(wt[...], x1_ref[...])
    collected = dot(rt[...], g1_ref[...])
    decay = dot(ends[...], spread)[:8]
    for pair in range(wide // LANES):
        lanes = slice(pair * LANES, (pair + 1) * LANES)
        out_ref[pair, :state] = written[:, lanes]
        out_ref[pair, state : 2 * state] = collected[:, lanes]
        out_ref[pair, 2 * state :] = decay[:, lanes]


def scan_kernel(in_ref, out_ref):
    shards = in_ref.shape[0]
    state = out_ref.shape[1] // 2
    carried = jnp.zeros((state, LANES), F32)
    for shard in range(shards):
        out_ref[shard, :state] = carried
        carried = in_ref[shard, 2 * state : 2 * state + 1] * carried + in_ref[shard, :state]
    carried = jnp.zeros((state, LANES), F32)
    for shard in reversed(range(shards)):
        out_ref[shard, state:] = carried
        carried = in_ref[shard, 2 * state : 2 * state + 1] * carried + in_ref[shard, state : 2 * state]


def local_kernel(
    x_ref, g_ref, w_ref, r_ref, ld_ref, gi_ref, out_ref, fa, fb, between, pw, wt, rt, xs, gs, acc, wrote, took, into_s, back_s
):
    heads, tokens = ld_ref.shape
    wide = x_ref.shape[1]
    head_size = wide * pl.num_programs(0) // heads
    count, state, _ = wt.shape
    step = pl.program_id(0)
    rows = lax.broadcasted_iota(jnp.int32, (SUB, SUB), 0)
    columns = lax.broadcasted_iota(jnp.int32, (SUB, SUB), 1)
    upper = columns >= rows

    @pl.when(step == 0)
    def _():
        sums = running_sums(jnp.concatenate([ld_ref[...]] * (LANES // heads), axis=0))
        middles = []
        afters = []
        for k in range(count):
            tok = slice(k * SUB, (k + 1) * SUB)
            middle = sums[k][MIDDLE : MIDDLE + 1]
            fa[tok] = two_terms(jnp.exp(middle - sums[k]), heads)
            fb[tok] = two_terms(jnp.exp(sums[k] - middle), heads)
            middles.append(middle)
            afters.append(sums[k][SUB - 1 :] - middle)
            write, read = w_ref[tok], r_ref[tok]
            pairs = jnp.where(upper, dot(write, read, ((1,), (1,))), 0.0).astype(BF16)
            pw[k] = jnp.concatenate([pairs, write], axis=1)
            wt[k] = write.T
            rt[k] = read.T
        into = [middles[0]] + [middles[k] + afters[k - 1] for k in range(1, count)]
        back = [afters[k] + middles[k + 1] for k in range(count - 1)] + [afters[count - 1]]
        between[...] = two_terms(jnp.exp(jnp.concatenate(into + back, axis=0)), heads)
        acc[...] = jnp.zeros_like(acc)

    spread = spread_matrix(heads, head_size, wide, step)
    factor = dot(between[...], spread)
    xs[...] = (x_ref[...].astype(F32) * dot(fa[...], spread)).astype(BF16)
    gs[...] = (g_ref[...].astype(F32) * dot(fb[...], spread)).astype(BF16)
    for k in range(count):
        tok = slice(k * SUB, (k + 1) * SUB)
        took[k] = dot(rt[k], gs[tok])
        wrote[k] = dot(wt[k], xs[tok])

    back = jnp.zeros((state, wide), F32)
    for k in reversed(range(count)):
        back_s[k] = back.astype(BF16)
        if k:
            back = factor[count + k - 1 : count + k] * (back + took[k])
    into = jnp.zeros((state, wide), F32)
    for k in range(count):
        into_s[k] = into.astype(BF16)
        if k + 1 < count:
            into = factor[k + 1 : k + 2] * (into + wrote[k])

    for k in range(count):
        tok = slice(k * SUB, (k + 1) * SUB)
        right = jnp.concatenate([gs[tok], back_s[k]], axis=0)
        left = jnp.concatenate([xs[tok], into_s[k]], axis=0)
        gi_ref[tok] = dot(fa[tok], spread) * dot(pw[k], right)
        acc[k] += dot(left, right, ((1,), (1,)))

    @pl.when(step == pl.num_programs(0) - 1)
    def _():
        for k in range(count):
            tok = slice(k * SUB, (k + 1) * SUB)
            weights = jnp.where(upper, acc[k, :SUB, :SUB], 0.0).astype(BF16)
            out_ref[k, :, :state] = dot(weights, r_ref[tok]) + acc[k, :SUB, SUB:]
            out_ref[k, :, state:] = (dot(wt[k], weights) + acc[k, SUB:, :SUB]).T


def meet_kernel(core_ref, x1_ref, g1_ref, st_ref, part_ref, mine_ref, other_ref, states):
    state = st_ref.shape[1] // 2
    core = core_ref[0]
    for p in range(st_ref.shape[0]):
        states[:, p * LANES : (p + 1) * LANES] = st_ref[p].astype(BF16)
    for out_ref, which in ((other_ref, 1 - core), (mine_ref, core)):
        for chip in range(out_ref.shape[0]):
            k = 2 * chip + which
            tok = pl.ds(pl.multiple_of(k * SUB, SUB), SUB)
            out_ref[chip, :, :state] = part_ref[k, :, :state] + dot(x1_ref[tok], states[state:], ((1,), (1,)))
            out_ref[chip, :, state:] = part_ref[k, :, state:] + dot(g1_ref[tok], states[:state], ((1,), (1,)))


def finish_kernel(gi_ref, st_ref, w_ref, fx, out_ref, *, heads):
    wide = gi_ref.shape[1]
    head_size = wide * pl.num_programs(0) // heads
    state = w_ref.shape[1]
    spread = spread_matrix(heads, head_size, wide, pl.program_id(0))
    leaving = jnp.concatenate([st_ref[p, state:].astype(BF16) for p in range(wide // LANES)], axis=1)
    for start in range(0, w_ref.shape[0], WIDE):
        tok = slice(start, start + WIDE)
        out_ref[tok] = (gi_ref[tok] + dot(fx[tok], spread) * dot(w_ref[tok], leaving)).astype(BF16)


def params(mib):
    return pltpu.CompilerParams(vmem_limit_bytes=mib * 2**20)


HERE = pl.BlockSpec(memory_space=pltpu.VMEM)


def fixed(*shape):
    return pl.BlockSpec(shape, lambda i: (0,) * len(shape))


def summarise(x, g, w, r, ld):
    tokens, width = x.shape
    state = w.shape[1]
    pairs = WIDE // LANES
    wide = pl.BlockSpec((tokens, WIDE), lambda i: (0, i))
    return pl.pallas_call(
        summary_kernel,
        grid=(width // WIDE,),
        in_specs=[wide, wide, fixed(tokens, state), fixed(tokens, state), fixed(*ld.shape)],
        out_specs=[
            pl.BlockSpec((pairs, 2 * state + 8, LANES), lambda i: (i, 0, 0)),
            wide,
            wide,
            fixed(tokens, LANES),
        ],
        out_shape=[
            jax.ShapeDtypeStruct((width // LANES, 2 * state + 8, LANES), F32),
            jax.ShapeDtypeStruct((tokens, width), BF16),
            jax.ShapeDtypeStruct((tokens, width), BF16),
            jax.ShapeDtypeStruct((tokens, LANES), BF16),
        ],
        scratch_shapes=[
            pltpu.VMEM((tokens, LANES), BF16),
            pltpu.VMEM((16, LANES), BF16),
            pltpu.VMEM((state, tokens), BF16),
            pltpu.VMEM((state, tokens), BF16),
        ],
        compiler_params=params(60),
        name="summary",
    )(x, g, w, r, ld)


def scan_shards(every):
    return pl.pallas_call(
        scan_kernel,
        in_specs=[HERE],
        out_specs=HERE,
        out_shape=jax.ShapeDtypeStruct((every.shape[0], every.shape[1] - 8, LANES), F32),
        compiler_params=params(16),
        name="scan",
    )(every)


def local_gradients(x, g, w, r, ld):
    tokens, width = x.shape
    state = w.shape[1]
    count = tokens // SUB
    wide = pl.BlockSpec((tokens, WIDE), lambda i: (0, i))
    return pl.pallas_call(
        local_kernel,
        grid=(width // WIDE,),
        in_specs=[wide, wide, fixed(tokens, state), fixed(tokens, state), fixed(*ld.shape)],
        out_specs=[wide, fixed(count, SUB, 2 * state)],
        out_shape=[
            jax.ShapeDtypeStruct((tokens, width), F32),
            jax.ShapeDtypeStruct((count, SUB, 2 * state), F32),
        ],
        scratch_shapes=[
            pltpu.VMEM((tokens, LANES), BF16),
            pltpu.VMEM((tokens, LANES), BF16),
            pltpu.VMEM((2 * count, LANES), BF16),
            pltpu.VMEM((count, SUB, SUB + state), BF16),
            pltpu.VMEM((count, state, SUB), BF16),
            pltpu.VMEM((count, state, SUB), BF16),
            pltpu.VMEM((tokens, WIDE), BF16),
            pltpu.VMEM((tokens, WIDE), BF16),
            pltpu.VMEM((count, SUB + state, SUB + state), F32),
            pltpu.VMEM((count, state, WIDE), F32),
            pltpu.VMEM((count, state, WIDE), F32),
            pltpu.VMEM((count, state, WIDE), BF16),
            pltpu.VMEM((count, state, WIDE), BF16),
        ],
        compiler_params=params(36),
        cost_estimate=pl.CostEstimate(flops=8 * 10**9, bytes_accessed=17 * 10**6, transcendentals=0),
        name="local",
    )(x, g, w, r, ld)


def meet(core, x1, g1, own, parts):
    tokens, width = x1.shape
    count, _, both = parts.shape
    half = jax.ShapeDtypeStruct((count // 2, SUB, both), F32)
    return pl.pallas_call(
        meet_kernel,
        in_specs=[pl.BlockSpec(memory_space=pltpu.SMEM)] + [HERE] * 4,
        out_specs=[HERE, HERE],
        out_shape=[half, half],
        scratch_shapes=[pltpu.VMEM((both, width), BF16)],
        compiler_params=params(16),
        name="meet",
    )(core, x1, g1, own, parts)


def finish(gi, own, w, fx, heads):
    tokens, width = gi.shape
    state = w.shape[1]
    pairs = WIDE // LANES
    wide = pl.BlockSpec((tokens, WIDE), lambda i: (0, i))

    def kernel(*refs):
        finish_kernel(*refs, heads=heads)

    return pl.pallas_call(
        kernel,
        grid=(width // WIDE,),
        in_specs=[
            wide,
            pl.BlockSpec((pairs, 2 * state, LANES), lambda i: (i, 0, 0)),
            fixed(tokens, state),
            fixed(tokens, LANES),
        ],
        out_specs=wide,
        out_shape=jax.ShapeDtypeStruct((tokens, width), BF16),
        compiler_params=params(24),
        cost_estimate=pl.CostEstimate(flops=2 * 10**9, bytes_accessed=13 * 10**6, transcendentals=0),
        name="finish",
    )(gi, own, w, fx)


def body(scaled_input, out_grad, write_proj, read_proj, log_decay):
    heads = log_decay.shape[0]
    state = write_proj.shape[1]
    ranks = lax.axis_size("head")
    rank = lax.axis_index("head")
    summary, x1, g1, fx = summarise(scaled_input, out_grad, write_proj, read_proj, log_decay)
    every = lax.all_to_all(summary, "seq", 0, 0, tiled=True)
    gi, parts = local_gradients(scaled_input, out_grad, write_proj, read_proj, log_decay)
    own = lax.all_to_all(scan_shards(every), "seq", 0, 0, tiled=True)
    mine, other = meet((rank % 2).astype(jnp.int32).reshape(1), x1, g1, own, parts)
    chip = mine + lax.ppermute(other, "head", [(i, i ^ 1) for i in range(ranks)])
    groups = [list(range(core, ranks, 2)) for core in range(2)]
    shared = lax.all_to_all(chip, "head", 0, 0, axis_index_groups=groups, tiled=True).sum(axis=0)
    grad_input = finish(gi, own, write_proj, fx, heads)
    return grad_input, shared[:, :state].astype(BF16), shared[:, state:].astype(BF16)


def solution(mesh):
    return jax.shard_map(
        body,
        mesh=mesh,
        in_specs=(
            P("seq", "head"),
            P("seq", "head"),
            P("seq", None),
            P("seq", None),
            P("head", "seq"),
        ),
        out_specs=(P("seq", "head"), P(("seq", "head"), None), P(("seq", "head"), None)),
        check_vma=False,
    )
```

```python
import jax
import jax.numpy as jnp
from jax import lax
from jax.experimental import pallas as pl
from jax.experimental.pallas import tpu as pltpu
from jax.sharding import PartitionSpec as P

SUB = 128
LANES = 128
WIDE = 512
FIRST = 1024
MIDDLE = SUB // 2 - 1
F32 = jnp.float32
BF16 = jnp.bfloat16


def dot(a, b, dims=((1,), (0,))):
    return lax.dot_general(a, b, (dims, ((), ())), preferred_element_type=F32)


def running_sums(decays):
    rows = lax.broadcasted_iota(jnp.int32, (SUB, SUB), 0)
    columns = lax.broadcasted_iota(jnp.int32, (SUB, SUB), 1)
    lower = jnp.where(rows >= columns, 1.0, 0.0).astype(BF16)
    first = decays.astype(BF16)
    left = decays - first.astype(F32)
    second = left.astype(BF16)
    third = (left - second.astype(F32)).astype(BF16)
    sums = []
    for start in range(0, decays.shape[1], SUB):
        tok = slice(start, start + SUB)
        a, b, c = (dot(lower, term[:, tok], ((1,), (1,))) for term in (first, second, third))
        sums.append(a + (b + c))
    return sums


def two_terms(values, heads):
    lane = lax.broadcasted_iota(jnp.int32, values.shape, 1)
    high = values.astype(BF16).astype(F32)
    kept = jnp.where(lane < heads, high, jnp.where(lane < 2 * heads, values - high, 0.0))
    return kept.astype(BF16)


def spread_matrix(heads, head_size, wide, step):
    row = lax.broadcasted_iota(jnp.int32, (LANES, wide), 0)
    column = lax.broadcasted_iota(jnp.int32, (LANES, wide), 1)
    same = lax.rem(row, heads) == (step * wide + column) // head_size
    return jnp.where(same, 1.0, 0.0).astype(BF16)


def summary_kernel(x_hbm, g_hbm, w_hbm, r_hbm, ld_hbm, out_hbm, fx, fg, ends, wt, rt, xb, gb, w_ref, r_ref, ld_ref, out_ref, sems):
    heads, tokens = ld_ref.shape
    steps, _, wide = xb.shape
    head_size = wide * steps // heads
    state = w_ref.shape[1]
    pairs = wide // LANES

    def load(source, target, step, sem):
        columns = pl.ds(pl.multiple_of(step * wide, wide), wide)
        return pltpu.make_async_copy(source.at[:, columns], target.at[step], sems.at[sem])

    def save(step):
        slots = pl.ds(step * pairs, pairs)
        return pltpu.make_async_copy(out_ref.at[slots], out_hbm.at[slots], sems.at[2 * steps + step])

    small = [
        pltpu.make_async_copy(source, target, sems.at[3 * steps + n])
        for n, (source, target) in enumerate(((ld_hbm, ld_ref), (w_hbm, w_ref), (r_hbm, r_ref)))
    ]
    for copy in small:
        copy.start()
    for step in range(steps):
        load(x_hbm, xb, step, step).start()
        load(g_hbm, gb, step, steps + step).start()

    small[0].wait()
    sums = running_sums(jnp.concatenate([ld_ref[...]] * (LANES // heads), axis=0))
    before = jnp.zeros((1, LANES), F32)
    for k in range(len(sums)):
        sums[k] = sums[k] + before
        before = sums[k][SUB - 1 :]
    for k in range(len(sums)):
        tok = slice(k * SUB, (k + 1) * SUB)
        fx[tok] = two_terms(jnp.exp(before - sums[k]), heads)
        fg[tok] = two_terms(jnp.exp(sums[k]), heads)
    ends[...] = two_terms(jnp.exp(jnp.broadcast_to(before, ends.shape)), heads)
    small[1].wait()
    small[2].wait()
    for start in range(0, tokens, SUB):
        tok = slice(start, start + SUB)
        wt[:, tok] = w_ref[tok].T
        rt[:, tok] = r_ref[tok].T

    for step in range(steps):
        spread = spread_matrix(heads, head_size, wide, step)
        load(x_hbm, xb, step, step).wait()
        written = dot(wt[...], (xb[step].astype(F32) * dot(fx[...], spread)).astype(BF16))
        load(g_hbm, gb, step, steps + step).wait()
        collected = dot(rt[...], (gb[step].astype(F32) * dot(fg[...], spread)).astype(BF16))
        decay = dot(ends[...], spread)[:8]
        for pair in range(pairs):
            lanes = slice(pair * LANES, (pair + 1) * LANES)
            out_ref[step * pairs + pair, :state] = written[:, lanes]
            out_ref[step * pairs + pair, state : 2 * state] = collected[:, lanes]
            out_ref[step * pairs + pair, 2 * state :] = decay[:, lanes]
        save(step).start()
    for step in range(steps):
        save(step).wait()


def scan_kernel(in_ref, out_hbm, out_ref, sems):
    shards = in_ref.shape[0]
    state = out_ref.shape[1] // 2
    carried = jnp.zeros((state, LANES), F32)
    for shard in range(shards):
        out_ref[shard, :state] = carried
        carried = in_ref[shard, 2 * state : 2 * state + 1] * carried + in_ref[shard, :state]
    carried = jnp.zeros((state, LANES), F32)
    copies = []
    for shard in reversed(range(shards)):
        out_ref[shard, state:] = carried
        carried = in_ref[shard, 2 * state : 2 * state + 1] * carried + in_ref[shard, state : 2 * state]
        copies.append(pltpu.make_async_copy(out_ref.at[shard], out_hbm.at[shard], sems.at[shard]))
        copies[-1].start()
    for copy in copies:
        copy.wait()


def local_kernel(
    x_ref, g_ref, w_ref, r_ref, ld_ref, gi_ref, out_ref, x1_ref, g1_ref, fx, fa, fb, fg, between, pw, wt, rt, xs, gs, acc, wrote, took, into_s, back_s
):
    heads, tokens = ld_ref.shape
    wide = x_ref.shape[1]
    head_size = wide * pl.num_programs(0) // heads
    count, state, _ = wt.shape
    step = pl.program_id(0)
    rows = lax.broadcasted_iota(jnp.int32, (SUB, SUB), 0)
    columns = lax.broadcasted_iota(jnp.int32, (SUB, SUB), 1)
    upper = columns >= rows

    @pl.when(step == 0)
    def _():
        sums = running_sums(jnp.concatenate([ld_ref[...]] * (LANES // heads), axis=0))
        before = jnp.zeros((1, LANES), F32)
        middles = []
        afters = []
        for k in range(count):
            tok = slice(k * SUB, (k + 1) * SUB)
            middle = sums[k][MIDDLE : MIDDLE + 1]
            fa[tok] = two_terms(jnp.exp(middle - sums[k]), heads)
            fb[tok] = two_terms(jnp.exp(sums[k] - middle), heads)
            middles.append(middle)
            afters.append(sums[k][SUB - 1 :] - middle)
            sums[k] = sums[k] + before
            before = sums[k][SUB - 1 :]
            write, read = w_ref[tok], r_ref[tok]
            pairs = jnp.where(upper, dot(write, read, ((1,), (1,))), 0.0).astype(BF16)
            pw[k] = jnp.concatenate([pairs, write], axis=1)
            wt[k] = write.T
            rt[k] = read.T
        into = [middles[0]] + [middles[k] + afters[k - 1] for k in range(1, count)]
        back = [afters[k] + middles[k + 1] for k in range(count - 1)] + [afters[count - 1]]
        between[...] = two_terms(jnp.exp(jnp.concatenate(into + back, axis=0)), heads)
        for k in range(count):
            tok = slice(k * SUB, (k + 1) * SUB)
            fx[tok] = two_terms(jnp.exp(before - sums[k]), heads)
            fg[tok] = two_terms(jnp.exp(sums[k]), heads)
        acc[...] = jnp.zeros_like(acc)

    spread = spread_matrix(heads, head_size, wide, step)
    factor = dot(between[...], spread)
    x1_ref[...] = (x_ref[...].astype(F32) * dot(fx[...], spread)).astype(BF16)
    g1_ref[...] = (g_ref[...].astype(F32) * dot(fg[...], spread)).astype(BF16)
    xs[...] = (x_ref[...].astype(F32) * dot(fa[...], spread)).astype(BF16)
    gs[...] = (g_ref[...].astype(F32) * dot(fb[...], spread)).astype(BF16)
    for k in range(count):
        tok = slice(k * SUB, (k + 1) * SUB)
        took[k] = dot(rt[k], gs[tok])
        wrote[k] = dot(wt[k], xs[tok])

    back = jnp.zeros((state, wide), F32)
    for k in reversed(range(count)):
        back_s[k] = back.astype(BF16)
        if k:
            back = factor[count + k - 1 : count + k] * (back + took[k])
    into = jnp.zeros((state, wide), F32)
    for k in range(count):
        into_s[k] = into.astype(BF16)
        if k + 1 < count:
            into = factor[k + 1 : k + 2] * (into + wrote[k])

    for k in range(count):
        tok = slice(k * SUB, (k + 1) * SUB)
        right = jnp.concatenate([gs[tok], back_s[k]], axis=0)
        left = jnp.concatenate([xs[tok], into_s[k]], axis=0)
        gi_ref[tok] = dot(fa[tok], spread) * dot(pw[k], right)
        acc[k] += dot(left, right, ((1,), (1,)))

    @pl.when(step == pl.num_programs(0) - 1)
    def _():
        for k in range(count):
            tok = slice(k * SUB, (k + 1) * SUB)
            weights = jnp.where(upper, acc[k, :SUB, :SUB], 0.0).astype(BF16)
            out_ref[k, :, :state] = dot(weights, r_ref[tok]) + acc[k, :SUB, SUB:]
            out_ref[k, :, state:] = (dot(wt[k], weights) + acc[k, SUB:, :SUB]).T


def meet_kernel(core_ref, x1_hbm, g1_hbm, part_hbm, st_ref, out_ref, *rest, first):
    states = rest[0] if first else st_ref
    x1, g1, part, sems = rest[-4:]
    chips = out_ref.shape[0]
    state = states.shape[0] // 2
    which = 1 - core_ref[0] if first else core_ref[0]

    def load(chip):
        k = 2 * chip + which
        tok = pl.ds(pl.multiple_of(k * SUB, SUB), SUB)
        return (
            pltpu.make_async_copy(x1_hbm.at[tok], x1.at[chip], sems.at[chip]),
            pltpu.make_async_copy(g1_hbm.at[tok], g1.at[chip], sems.at[chips + chip]),
            pltpu.make_async_copy(part_hbm.at[k], part.at[chip], sems.at[2 * chips + chip]),
        )

    for chip in range(chips):
        for copy in load(chip):
            copy.start()
    if first:
        for p in range(st_ref.shape[0]):
            states[:, p * LANES : (p + 1) * LANES] = st_ref[p].astype(BF16)
    for chip in range(chips):
        for copy in load(chip):
            copy.wait()
        out_ref[chip, :, :state] = part[chip, :, :state] + dot(x1[chip], states[state:], ((1,), (1,)))
        out_ref[chip, :, state:] = part[chip, :, state:] + dot(g1[chip], states[:state], ((1,), (1,)))


def finish_kernel(gi_ref, st_ref, w_ref, fx, out_ref, *, heads):
    wide = gi_ref.shape[1]
    head_size = wide * pl.num_programs(0) // heads
    state = w_ref.shape[1]
    spread = spread_matrix(heads, head_size, wide, pl.program_id(0))
    leaving = jnp.concatenate([st_ref[p, state:].astype(BF16) for p in range(wide // LANES)], axis=1)
    for start in range(0, w_ref.shape[0], WIDE):
        tok = slice(start, start + WIDE)
        out_ref[tok] = (gi_ref[tok] + dot(fx[tok], spread) * dot(w_ref[tok], leaving)).astype(BF16)


def params(mib):
    return pltpu.CompilerParams(vmem_limit_bytes=mib * 2**20)


def in_hbm(array):
    return pltpu.with_memory_space_constraint(array, pltpu.HBM)


HERE = pl.BlockSpec(memory_space=pltpu.VMEM)


def fixed(*shape):
    return pl.BlockSpec(shape, lambda i: (0,) * len(shape))


def summarise(x, g, w, r, ld):
    tokens, width = x.shape
    state = w.shape[1]
    steps = width // FIRST
    there = pl.BlockSpec(memory_space=pltpu.HBM)
    payload = (width // LANES, 2 * state + 8, LANES)
    return pl.pallas_call(
        summary_kernel,
        in_specs=[there] * 5,
        out_specs=there,
        out_shape=jax.ShapeDtypeStruct(payload, F32),
        scratch_shapes=[
            pltpu.VMEM((tokens, LANES), BF16),
            pltpu.VMEM((tokens, LANES), BF16),
            pltpu.VMEM((16, LANES), BF16),
            pltpu.VMEM((state, tokens), BF16),
            pltpu.VMEM((state, tokens), BF16),
            pltpu.VMEM((steps, tokens, FIRST), BF16),
            pltpu.VMEM((steps, tokens, FIRST), BF16),
            pltpu.VMEM((tokens, state), BF16),
            pltpu.VMEM((tokens, state), BF16),
            pltpu.VMEM(ld.shape, F32),
            pltpu.VMEM(payload, F32),
            pltpu.SemaphoreType.DMA((3 * steps + 3,)),
        ],
        compiler_params=params(60),
        name="summary",
    )(x, g, w, r, ld)


def scan_shards(every):
    shards = every.shape[0]
    shape = (shards, every.shape[1] - 8, LANES)
    return pl.pallas_call(
        scan_kernel,
        in_specs=[HERE],
        out_specs=pl.BlockSpec(memory_space=pltpu.HBM),
        out_shape=pltpu.HBM(shape, F32),
        scratch_shapes=[pltpu.VMEM(shape, F32), pltpu.SemaphoreType.DMA((shards,))],
        compiler_params=params(16),
        name="scan",
    )(every)


def local_gradients(x, g, w, r, ld):
    tokens, width = x.shape
    state = w.shape[1]
    count = tokens // SUB
    wide = pl.BlockSpec((tokens, WIDE), lambda i: (0, i))
    return pl.pallas_call(
        local_kernel,
        grid=(width // WIDE,),
        in_specs=[wide, wide, fixed(tokens, state), fixed(tokens, state), fixed(*ld.shape)],
        out_specs=[wide, fixed(count, SUB, 2 * state), wide, wide, fixed(tokens, LANES)],
        out_shape=[
            pltpu.HBM((tokens, width), F32),
            pltpu.HBM((count, SUB, 2 * state), F32),
            pltpu.HBM((tokens, width), BF16),
            pltpu.HBM((tokens, width), BF16),
            pltpu.HBM((tokens, LANES), BF16),
        ],
        scratch_shapes=[
            pltpu.VMEM((tokens, LANES), BF16),
            pltpu.VMEM((tokens, LANES), BF16),
            pltpu.VMEM((tokens, LANES), BF16),
            pltpu.VMEM((2 * count, LANES), BF16),
            pltpu.VMEM((count, SUB, SUB + state), BF16),
            pltpu.VMEM((count, state, SUB), BF16),
            pltpu.VMEM((count, state, SUB), BF16),
            pltpu.VMEM((tokens, WIDE), BF16),
            pltpu.VMEM((tokens, WIDE), BF16),
            pltpu.VMEM((count, SUB + state, SUB + state), F32),
            pltpu.VMEM((count, state, WIDE), F32),
            pltpu.VMEM((count, state, WIDE), F32),
            pltpu.VMEM((count, state, WIDE), BF16),
            pltpu.VMEM((count, state, WIDE), BF16),
        ],
        compiler_params=params(60),
        cost_estimate=pl.CostEstimate(flops=10**10, bytes_accessed=26 * 10**6, transcendentals=0),
        name="local",
    )(in_hbm(x), in_hbm(g), w, r, ld)


def meet(core, x1, g1, parts, states, first):
    tokens, width = x1.shape
    count, _, both = parts.shape
    chips = count // 2

    def kernel(*refs):
        meet_kernel(*refs, first=first)

    return pl.pallas_call(
        kernel,
        in_specs=[pl.BlockSpec(memory_space=pltpu.SMEM)] + [pl.BlockSpec(memory_space=pltpu.HBM)] * 3 + [HERE],
        out_specs=[HERE] * (1 + first),
        out_shape=[
            jax.ShapeDtypeStruct((chips, SUB, both), F32),
            jax.ShapeDtypeStruct((both, width), BF16),
        ][: 1 + first],
        scratch_shapes=[
            pltpu.VMEM((chips, SUB, width), BF16),
            pltpu.VMEM((chips, SUB, width), BF16),
            pltpu.VMEM((chips, SUB, both), F32),
            pltpu.SemaphoreType.DMA((3 * chips,)),
        ],
        compiler_params=params(24),
        cost_estimate=pl.CostEstimate(flops=10**9, bytes_accessed=4 * 10**6, transcendentals=0),
        name="meet_other" if first else "meet_mine",
    )(core, in_hbm(x1), in_hbm(g1), in_hbm(parts), states)


def finish(gi, own, w, fx, heads):
    tokens, width = gi.shape
    state = w.shape[1]
    pairs = WIDE // LANES
    wide = pl.BlockSpec((tokens, WIDE), lambda i: (0, i))

    def kernel(*refs):
        finish_kernel(*refs, heads=heads)

    return pl.pallas_call(
        kernel,
        grid=(width // WIDE,),
        in_specs=[
            wide,
            pl.BlockSpec((pairs, 2 * state, LANES), lambda i: (i, 0, 0)),
            fixed(tokens, state),
            fixed(tokens, LANES),
        ],
        out_specs=wide,
        out_shape=jax.ShapeDtypeStruct((tokens, width), BF16),
        compiler_params=params(40),
        cost_estimate=pl.CostEstimate(flops=2 * 10**9, bytes_accessed=13 * 10**6, transcendentals=0),
        name="finish",
    )(in_hbm(gi), own, w, fx)


def body(scaled_input, out_grad, write_proj, read_proj, log_decay):
    heads = log_decay.shape[0]
    state = write_proj.shape[1]
    ranks = lax.axis_size("head")
    core = (lax.axis_index("head") % 2).astype(jnp.int32).reshape(1)
    every = lax.all_to_all(
        summarise(scaled_input, out_grad, write_proj, read_proj, log_decay), "seq", 0, 0, tiled=True
    )
    gi, parts, x1, g1, fx = local_gradients(scaled_input, out_grad, write_proj, read_proj, log_decay)
    own = lax.all_to_all(scan_shards(every), "seq", 0, 0, tiled=True)
    other, states = meet(core, x1, g1, parts, own, True)
    arrived = lax.ppermute(other, "head", [(i, i ^ 1) for i in range(ranks)])
    (mine,) = meet(core, x1, g1, parts, states, False)
    groups = [list(range(first, ranks, 2)) for first in range(2)]
    shared = lax.all_to_all(mine + arrived, "head", 0, 0, axis_index_groups=groups, tiled=True).sum(axis=0)
    grad_input = finish(gi, own, write_proj, fx, heads)
    return grad_input, shared[:, :state].astype(BF16), shared[:, state:].astype(BF16)


def solution(mesh):
    return jax.shard_map(
        body,
        mesh=mesh,
        in_specs=(
            P("seq", "head"),
            P("seq", "head"),
            P("seq", None),
            P("seq", None),
            P("head", "seq"),
        ),
        out_specs=(P("seq", "head"), P(("seq", "head"), None), P(("seq", "head"), None)),
        check_vma=False,
    )
```

```python
import jax
import jax.numpy as jnp
from jax import lax
from jax.experimental import pallas as pl
from jax.experimental.pallas import tpu as pltpu
from jax.sharding import PartitionSpec as P

SUB = 128
LANES = 128
WIDE = 512
FIRST = 1024
MIDDLE = SUB // 2 - 1
F32 = jnp.float32
BF16 = jnp.bfloat16


def dot(a, b, dims=((1,), (0,))):
    return lax.dot_general(a, b, (dims, ((), ())), preferred_element_type=F32)


def running_sums(decays):
    rows = lax.broadcasted_iota(jnp.int32, (SUB, SUB), 0)
    columns = lax.broadcasted_iota(jnp.int32, (SUB, SUB), 1)
    lower = jnp.where(rows >= columns, 1.0, 0.0).astype(BF16)
    first = decays.astype(BF16)
    left = decays - first.astype(F32)
    second = left.astype(BF16)
    third = (left - second.astype(F32)).astype(BF16)
    sums = []
    for start in range(0, decays.shape[1], SUB):
        tok = slice(start, start + SUB)
        a, b, c = (dot(lower, term[:, tok], ((1,), (1,))) for term in (first, second, third))
        sums.append(a + (b + c))
    return sums


def two_terms(values, heads):
    lane = lax.broadcasted_iota(jnp.int32, values.shape, 1)
    high = values.astype(BF16).astype(F32)
    kept = jnp.where(lane < heads, high, jnp.where(lane < 2 * heads, values - high, 0.0))
    return kept.astype(BF16)


def spread_matrix(heads, head_size, wide, step):
    row = lax.broadcasted_iota(jnp.int32, (LANES, wide), 0)
    column = lax.broadcasted_iota(jnp.int32, (LANES, wide), 1)
    same = lax.rem(row, heads) == (step * wide + column) // head_size
    return jnp.where(same, 1.0, 0.0).astype(BF16)


def summary_kernel(x_hbm, g_hbm, w_hbm, r_hbm, ld_hbm, out_hbm, fx, fg, ends, wt, rt, xb, gb, w_ref, r_ref, ld_ref, out_ref, sems):
    heads, tokens = ld_ref.shape
    steps, _, wide = xb.shape
    head_size = wide * steps // heads
    state = w_ref.shape[1]
    pairs = wide // LANES

    def load(source, target, step, sem):
        columns = pl.ds(pl.multiple_of(step * wide, wide), wide)
        return pltpu.make_async_copy(source.at[:, columns], target.at[step], sems.at[sem])

    def save(step):
        slots = pl.ds(step * pairs, pairs)
        return pltpu.make_async_copy(out_ref.at[slots], out_hbm.at[slots], sems.at[2 * steps + step])

    small = [
        pltpu.make_async_copy(source, target, sems.at[3 * steps + n])
        for n, (source, target) in enumerate(((ld_hbm, ld_ref), (w_hbm, w_ref), (r_hbm, r_ref)))
    ]
    for copy in small:
        copy.start()
    for step in range(steps):
        load(x_hbm, xb, step, step).start()
        load(g_hbm, gb, step, steps + step).start()

    small[0].wait()
    sums = running_sums(jnp.concatenate([ld_ref[...]] * (LANES // heads), axis=0))
    before = jnp.zeros((1, LANES), F32)
    for k in range(len(sums)):
        sums[k] = sums[k] + before
        before = sums[k][SUB - 1 :]
    for k in range(len(sums)):
        tok = slice(k * SUB, (k + 1) * SUB)
        fx[tok] = two_terms(jnp.exp(before - sums[k]), heads)
        fg[tok] = two_terms(jnp.exp(sums[k]), heads)
    ends[...] = two_terms(jnp.exp(jnp.broadcast_to(before, ends.shape)), heads)
    small[1].wait()
    small[2].wait()
    for start in range(0, tokens, SUB):
        tok = slice(start, start + SUB)
        wt[:, tok] = w_ref[tok].T
        rt[:, tok] = r_ref[tok].T

    for step in range(steps):
        spread = spread_matrix(heads, head_size, wide, step)
        load(x_hbm, xb, step, step).wait()
        written = dot(wt[...], (xb[step].astype(F32) * dot(fx[...], spread)).astype(BF16))
        load(g_hbm, gb, step, steps + step).wait()
        collected = dot(rt[...], (gb[step].astype(F32) * dot(fg[...], spread)).astype(BF16))
        decay = dot(ends[...], spread)[:8]
        for pair in range(pairs):
            lanes = slice(pair * LANES, (pair + 1) * LANES)
            out_ref[step * pairs + pair, :state] = written[:, lanes]
            out_ref[step * pairs + pair, state : 2 * state] = collected[:, lanes]
            out_ref[step * pairs + pair, 2 * state :] = decay[:, lanes]
        save(step).start()
    for step in range(steps):
        save(step).wait()


def scan_kernel(in_ref, out_ref):
    shards = in_ref.shape[0]
    state = out_ref.shape[1] // 2
    carried = jnp.zeros((state, LANES), F32)
    for shard in range(shards):
        out_ref[shard, :state] = carried
        carried = in_ref[shard, 2 * state : 2 * state + 1] * carried + in_ref[shard, :state]
    carried = jnp.zeros((state, LANES), F32)
    for shard in reversed(range(shards)):
        out_ref[shard, state:] = carried
        carried = in_ref[shard, 2 * state : 2 * state + 1] * carried + in_ref[shard, state : 2 * state]


def local_kernel(
    x_ref, g_ref, w_ref, r_ref, ld_ref, gi_ref, out_ref, x1_ref, g1_ref, fx, fa, fb, fg, between, pw, wt, rt, xs, gs, acc, wrote, took, into_s, back_s
):
    heads, tokens = ld_ref.shape
    wide = x_ref.shape[1]
    head_size = wide * pl.num_programs(0) // heads
    count, state, _ = wt.shape
    step = pl.program_id(0)
    rows = lax.broadcasted_iota(jnp.int32, (SUB, SUB), 0)
    columns = lax.broadcasted_iota(jnp.int32, (SUB, SUB), 1)
    upper = columns >= rows

    @pl.when(step == 0)
    def _():
        sums = running_sums(jnp.concatenate([ld_ref[...]] * (LANES // heads), axis=0))
        before = jnp.zeros((1, LANES), F32)
        middles = []
        afters = []
        for k in range(count):
            tok = slice(k * SUB, (k + 1) * SUB)
            middle = sums[k][MIDDLE : MIDDLE + 1]
            fa[tok] = two_terms(jnp.exp(middle - sums[k]), heads)
            fb[tok] = two_terms(jnp.exp(sums[k] - middle), heads)
            middles.append(middle)
            afters.append(sums[k][SUB - 1 :] - middle)
            sums[k] = sums[k] + before
            before = sums[k][SUB - 1 :]
            write, read = w_ref[tok], r_ref[tok]
            pairs = jnp.where(upper, dot(write, read, ((1,), (1,))), 0.0).astype(BF16)
            pw[k] = jnp.concatenate([pairs, write], axis=1)
            wt[k] = write.T
            rt[k] = read.T
        into = [middles[0]] + [middles[k] + afters[k - 1] for k in range(1, count)]
        back = [afters[k] + middles[k + 1] for k in range(count - 1)] + [afters[count - 1]]
        between[...] = two_terms(jnp.exp(jnp.concatenate(into + back, axis=0)), heads)
        for k in range(count):
            tok = slice(k * SUB, (k + 1) * SUB)
            fx[tok] = two_terms(jnp.exp(before - sums[k]), heads)
            fg[tok] = two_terms(jnp.exp(sums[k]), heads)
        acc[...] = jnp.zeros_like(acc)

    spread = spread_matrix(heads, head_size, wide, step)
    factor = dot(between[...], spread)
    x1_ref[...] = (x_ref[...].astype(F32) * dot(fx[...], spread)).astype(BF16)
    g1_ref[...] = (g_ref[...].astype(F32) * dot(fg[...], spread)).astype(BF16)
    xs[...] = (x_ref[...].astype(F32) * dot(fa[...], spread)).astype(BF16)
    gs[...] = (g_ref[...].astype(F32) * dot(fb[...], spread)).astype(BF16)
    for k in range(count):
        tok = slice(k * SUB, (k + 1) * SUB)
        took[k] = dot(rt[k], gs[tok])
        wrote[k] = dot(wt[k], xs[tok])

    back = jnp.zeros((state, wide), F32)
    for k in reversed(range(count)):
        back_s[k] = back.astype(BF16)
        if k:
            back = factor[count + k - 1 : count + k] * (back + took[k])
    into = jnp.zeros((state, wide), F32)
    for k in range(count):
        into_s[k] = into.astype(BF16)
        if k + 1 < count:
            into = factor[k + 1 : k + 2] * (into + wrote[k])

    for k in range(count):
        tok = slice(k * SUB, (k + 1) * SUB)
        right = jnp.concatenate([gs[tok], back_s[k]], axis=0)
        left = jnp.concatenate([xs[tok], into_s[k]], axis=0)
        gi_ref[tok] = dot(fa[tok], spread) * dot(pw[k], right)
        acc[k] += dot(left, right, ((1,), (1,)))

    @pl.when(step == pl.num_programs(0) - 1)
    def _():
        for k in range(count):
            tok = slice(k * SUB, (k + 1) * SUB)
            weights = jnp.where(upper, acc[k, :SUB, :SUB], 0.0).astype(BF16)
            out_ref[k, :, :state] = dot(weights, r_ref[tok]) + acc[k, :SUB, SUB:]
            out_ref[k, :, state:] = (dot(wt[k], weights) + acc[k, SUB:, :SUB]).T


def meet_half(place_ref, away, x1_ref, g1_ref, states, part_ref, out_ref):
    state = states.shape[0] // 2
    chips = out_ref.shape[0]
    core = 1 - place_ref[1] if away else place_ref[1]
    for slot in range(chips):
        k = 2 * lax.rem(place_ref[0] + slot, chips) + core
        tok = pl.ds(pl.multiple_of(k * SUB, SUB), SUB)
        out_ref[slot, :, :state] = part_ref[k, :, :state] + dot(x1_ref[tok], states[state:], ((1,), (1,)))
        out_ref[slot, :, state:] = part_ref[k, :, state:] + dot(g1_ref[tok], states[:state], ((1,), (1,)))


def meet_other_kernel(place_ref, x1_ref, g1_ref, st_ref, part_ref, out_ref, states):
    for p in range(st_ref.shape[0]):
        states[:, p * LANES : (p + 1) * LANES] = st_ref[p].astype(BF16)
    meet_half(place_ref, True, x1_ref, g1_ref, states, part_ref, out_ref)


def meet_mine_kernel(place_ref, x1_ref, g1_ref, states, part_ref, out_ref):
    meet_half(place_ref, False, x1_ref, g1_ref, states, part_ref, out_ref)


def finish_kernel(gi_ref, st_ref, w_ref, fx, out_ref, *, heads):
    wide = gi_ref.shape[1]
    head_size = wide * pl.num_programs(0) // heads
    state = w_ref.shape[1]
    spread = spread_matrix(heads, head_size, wide, pl.program_id(0))
    leaving = jnp.concatenate([st_ref[p, state:].astype(BF16) for p in range(wide // LANES)], axis=1)
    for start in range(0, w_ref.shape[0], WIDE):
        tok = slice(start, start + WIDE)
        out_ref[tok] = (gi_ref[tok] + dot(fx[tok], spread) * dot(w_ref[tok], leaving)).astype(BF16)


def params(mib):
    return pltpu.CompilerParams(vmem_limit_bytes=mib * 2**20)


def in_hbm(array):
    return pltpu.with_memory_space_constraint(array, pltpu.HBM)


HERE = pl.BlockSpec(memory_space=pltpu.VMEM)


def fixed(*shape):
    return pl.BlockSpec(shape, lambda i: (0,) * len(shape))


def summarise(x, g, w, r, ld):
    tokens, width = x.shape
    state = w.shape[1]
    steps = width // FIRST
    there = pl.BlockSpec(memory_space=pltpu.HBM)
    payload = (width // LANES, 2 * state + 8, LANES)
    return pl.pallas_call(
        summary_kernel,
        in_specs=[there] * 5,
        out_specs=there,
        out_shape=jax.ShapeDtypeStruct(payload, F32),
        scratch_shapes=[
            pltpu.VMEM((tokens, LANES), BF16),
            pltpu.VMEM((tokens, LANES), BF16),
            pltpu.VMEM((16, LANES), BF16),
            pltpu.VMEM((state, tokens), BF16),
            pltpu.VMEM((state, tokens), BF16),
            pltpu.VMEM((steps, tokens, FIRST), BF16),
            pltpu.VMEM((steps, tokens, FIRST), BF16),
            pltpu.VMEM((tokens, state), BF16),
            pltpu.VMEM((tokens, state), BF16),
            pltpu.VMEM(ld.shape, F32),
            pltpu.VMEM(payload, F32),
            pltpu.SemaphoreType.DMA((3 * steps + 3,)),
        ],
        compiler_params=params(60),
        name="summary",
    )(x, g, w, r, ld)


def scan_shards(every):
    return pl.pallas_call(
        scan_kernel,
        in_specs=[HERE],
        out_specs=HERE,
        out_shape=jax.ShapeDtypeStruct((every.shape[0], every.shape[1] - 8, LANES), F32),
        compiler_params=params(16),
        name="scan",
    )(every)


def local_gradients(x, g, w, r, ld):
    tokens, width = x.shape
    state = w.shape[1]
    count = tokens // SUB
    wide = pl.BlockSpec((tokens, WIDE), lambda i: (0, i))
    return pl.pallas_call(
        local_kernel,
        grid=(width // WIDE,),
        in_specs=[wide, wide, fixed(tokens, state), fixed(tokens, state), fixed(*ld.shape)],
        out_specs=[wide, fixed(count, SUB, 2 * state), wide, wide, fixed(tokens, LANES)],
        out_shape=[
            pltpu.HBM((tokens, width), F32),
            pltpu.HBM((count, SUB, 2 * state), F32),
            pltpu.HBM((tokens, width), BF16),
            pltpu.HBM((tokens, width), BF16),
            pltpu.HBM((tokens, LANES), BF16),
        ],
        scratch_shapes=[
            pltpu.VMEM((tokens, LANES), BF16),
            pltpu.VMEM((tokens, LANES), BF16),
            pltpu.VMEM((tokens, LANES), BF16),
            pltpu.VMEM((2 * count, LANES), BF16),
            pltpu.VMEM((count, SUB, SUB + state), BF16),
            pltpu.VMEM((count, state, SUB), BF16),
            pltpu.VMEM((count, state, SUB), BF16),
            pltpu.VMEM((tokens, WIDE), BF16),
            pltpu.VMEM((tokens, WIDE), BF16),
            pltpu.VMEM((count, SUB + state, SUB + state), F32),
            pltpu.VMEM((count, state, WIDE), F32),
            pltpu.VMEM((count, state, WIDE), F32),
            pltpu.VMEM((count, state, WIDE), BF16),
            pltpu.VMEM((count, state, WIDE), BF16),
        ],
        compiler_params=params(60),
        cost_estimate=pl.CostEstimate(flops=10**10, bytes_accessed=26 * 10**6, transcendentals=0),
        name="local",
    )(in_hbm(x), in_hbm(g), w, r, ld)


def meet(kernel, place, x1, g1, states, parts, keep):
    tokens, width = x1.shape
    count, _, both = parts.shape
    return pl.pallas_call(
        kernel,
        in_specs=[pl.BlockSpec(memory_space=pltpu.SMEM)] + [HERE] * 4,
        out_specs=[HERE] * (1 + keep),
        out_shape=[
            jax.ShapeDtypeStruct((count // 2, SUB, both), F32),
            jax.ShapeDtypeStruct((both, width), BF16),
        ][: 1 + keep],
        compiler_params=params(16),
        cost_estimate=pl.CostEstimate(flops=10**9, bytes_accessed=4 * 10**6, transcendentals=0),
        name="meet_other" if keep else "meet_mine",
    )(place, x1, g1, states, parts)


def finish(gi, own, w, fx, heads):
    tokens, width = gi.shape
    state = w.shape[1]
    pairs = WIDE // LANES
    wide = pl.BlockSpec((tokens, WIDE), lambda i: (0, i))

    def kernel(*refs):
        finish_kernel(*refs, heads=heads)

    return pl.pallas_call(
        kernel,
        grid=(width // WIDE,),
        in_specs=[
            wide,
            pl.BlockSpec((pairs, 2 * state, LANES), lambda i: (i, 0, 0)),
            fixed(tokens, state),
            fixed(tokens, LANES),
        ],
        out_specs=wide,
        out_shape=jax.ShapeDtypeStruct((tokens, width), BF16),
        compiler_params=params(40),
        cost_estimate=pl.CostEstimate(flops=2 * 10**9, bytes_accessed=13 * 10**6, transcendentals=0),
        name="finish",
    )(in_hbm(gi), own, w, fx)


def over_chips(terms):
    ranks = lax.axis_size("head")
    arrived = [
        lax.ppermute(terms[d], "head", [(i, (i + 2 * d) % ranks) for i in range(ranks)])
        for d in range(1, terms.shape[0])
    ]
    return sum(arrived, terms[0])


def body(scaled_input, out_grad, write_proj, read_proj, log_decay):
    heads = log_decay.shape[0]
    state = write_proj.shape[1]
    ranks = lax.axis_size("head")
    rank = lax.axis_index("head")
    place = jnp.stack([rank // 2, rank % 2]).astype(jnp.int32)
    every = lax.all_to_all(
        summarise(scaled_input, out_grad, write_proj, read_proj, log_decay), "seq", 0, 0, tiled=True
    )
    local = local_gradients(scaled_input, out_grad, write_proj, read_proj, log_decay)
    every, place, gi, parts, x1, g1, fx = lax.optimization_barrier((every, place, *local))
    own = lax.all_to_all(scan_shards(every), "seq", 0, 0, tiled=True)
    other, states = meet(meet_other_kernel, place, x1, g1, own, parts, True)
    arrived = lax.ppermute(other, "head", [(i, i ^ 1) for i in range(ranks)])
    (mine,) = meet(meet_mine_kernel, place, x1, g1, states, parts, False)
    shared = over_chips(mine + arrived)
    grad_input = finish(gi, own, write_proj, fx, heads)
    return grad_input, shared[:, :state].astype(BF16), shared[:, state:].astype(BF16)


def solution(mesh):
    return jax.shard_map(
        body,
        mesh=mesh,
        in_specs=(
            P("seq", "head"),
            P("seq", "head"),
            P("seq", None),
            P("seq", None),
            P("head", "seq"),
        ),
        out_specs=(P("seq", "head"), P(("seq", "head"), None), P(("seq", "head"), None)),
        check_vma=False,
    )
```

```python
import jax
import jax.numpy as jnp
from jax import lax
from jax.experimental import pallas as pl
from jax.experimental.pallas import tpu as pltpu
from jax.sharding import PartitionSpec as P

SUB = 128
LANES = 128
WIDE = 512
FIRST = 1024
MIDDLE = SUB // 2 - 1
F32 = jnp.float32
BF16 = jnp.bfloat16


def dot(a, b, dims=((1,), (0,))):
    return lax.dot_general(a, b, (dims, ((), ())), preferred_element_type=F32)


def running_sums(decays):
    rows = lax.broadcasted_iota(jnp.int32, (SUB, SUB), 0)
    columns = lax.broadcasted_iota(jnp.int32, (SUB, SUB), 1)
    lower = jnp.where(rows >= columns, 1.0, 0.0).astype(BF16)
    first = decays.astype(BF16)
    left = decays - first.astype(F32)
    second = left.astype(BF16)
    third = (left - second.astype(F32)).astype(BF16)
    sums = []
    for start in range(0, decays.shape[1], SUB):
        tok = slice(start, start + SUB)
        a, b, c = (dot(lower, term[:, tok], ((1,), (1,))) for term in (first, second, third))
        sums.append(a + (b + c))
    return sums


def two_terms(values, heads):
    lane = lax.broadcasted_iota(jnp.int32, values.shape, 1)
    high = values.astype(BF16).astype(F32)
    kept = jnp.where(lane < heads, high, jnp.where(lane < 2 * heads, values - high, 0.0))
    return kept.astype(BF16)


def spread_matrix(heads, head_size, wide, step):
    row = lax.broadcasted_iota(jnp.int32, (LANES, wide), 0)
    column = lax.broadcasted_iota(jnp.int32, (LANES, wide), 1)
    same = lax.rem(row, heads) == (step * wide + column) // head_size
    return jnp.where(same, 1.0, 0.0).astype(BF16)


def summary_kernel(x_hbm, g_hbm, w_hbm, r_hbm, ld_hbm, out_hbm, fx, fg, ends, wt, rt, xb, gb, w_ref, r_ref, ld_ref, out_ref, sems):
    heads, tokens = ld_ref.shape
    steps, _, wide = xb.shape
    head_size = wide * steps // heads
    state = w_ref.shape[1]
    pairs = wide // LANES

    def load(source, target, step, sem):
        columns = pl.ds(pl.multiple_of(step * wide, wide), wide)
        return pltpu.make_async_copy(source.at[:, columns], target.at[step], sems.at[sem])

    def save(step):
        slots = pl.ds(step * pairs, pairs)
        return pltpu.make_async_copy(out_ref.at[slots], out_hbm.at[slots], sems.at[2 * steps + step])

    small = [
        pltpu.make_async_copy(source, target, sems.at[3 * steps + n])
        for n, (source, target) in enumerate(((ld_hbm, ld_ref), (w_hbm, w_ref), (r_hbm, r_ref)))
    ]
    for copy in small:
        copy.start()
    for step in range(steps):
        load(x_hbm, xb, step, step).start()
        load(g_hbm, gb, step, steps + step).start()

    small[0].wait()
    sums = running_sums(jnp.concatenate([ld_ref[...]] * (LANES // heads), axis=0))
    before = jnp.zeros((1, LANES), F32)
    for k in range(len(sums)):
        sums[k] = sums[k] + before
        before = sums[k][SUB - 1 :]
    for k in range(len(sums)):
        tok = slice(k * SUB, (k + 1) * SUB)
        fx[tok] = two_terms(jnp.exp(before - sums[k]), heads)
        fg[tok] = two_terms(jnp.exp(sums[k]), heads)
    ends[...] = two_terms(jnp.exp(jnp.broadcast_to(before, ends.shape)), heads)
    small[1].wait()
    small[2].wait()
    for start in range(0, tokens, SUB):
        tok = slice(start, start + SUB)
        wt[:, tok] = w_ref[tok].T
        rt[:, tok] = r_ref[tok].T

    for step in range(steps):
        spread = spread_matrix(heads, head_size, wide, step)
        load(x_hbm, xb, step, step).wait()
        written = dot(wt[...], (xb[step].astype(F32) * dot(fx[...], spread)).astype(BF16))
        load(g_hbm, gb, step, steps + step).wait()
        collected = dot(rt[...], (gb[step].astype(F32) * dot(fg[...], spread)).astype(BF16))
        decay = dot(ends[...], spread)[:8]
        for pair in range(pairs):
            lanes = slice(pair * LANES, (pair + 1) * LANES)
            out_ref[step * pairs + pair, :state] = written[:, lanes]
            out_ref[step * pairs + pair, state : 2 * state] = collected[:, lanes]
            out_ref[step * pairs + pair, 2 * state :] = decay[:, lanes]
        save(step).start()
    for step in range(steps):
        save(step).wait()


def scan_kernel(in_ref, out_ref):
    shards = in_ref.shape[0]
    state = out_ref.shape[1] // 2
    carried = jnp.zeros((state, LANES), F32)
    for shard in range(shards):
        out_ref[shard, :state] = carried
        carried = in_ref[shard, 2 * state : 2 * state + 1] * carried + in_ref[shard, :state]
    carried = jnp.zeros((state, LANES), F32)
    for shard in reversed(range(shards)):
        out_ref[shard, state:] = carried
        carried = in_ref[shard, 2 * state : 2 * state + 1] * carried + in_ref[shard, state : 2 * state]


def local_kernel(
    x_ref, g_ref, w_ref, r_ref, ld_ref, gi_ref, out_ref, x1_ref, g1_ref, fx, fa, fb, fg, between, pw, wt, rt, xs, gs, acc, wrote, took, into_s, back_s
):
    heads, tokens = ld_ref.shape
    wide = x_ref.shape[1]
    head_size = wide * pl.num_programs(0) // heads
    count, state, _ = wt.shape
    step = pl.program_id(0)
    rows = lax.broadcasted_iota(jnp.int32, (SUB, SUB), 0)
    columns = lax.broadcasted_iota(jnp.int32, (SUB, SUB), 1)
    upper = columns >= rows

    @pl.when(step == 0)
    def _():
        sums = running_sums(jnp.concatenate([ld_ref[...]] * (LANES // heads), axis=0))
        before = jnp.zeros((1, LANES), F32)
        middles = []
        afters = []
        for k in range(count):
            tok = slice(k * SUB, (k + 1) * SUB)
            middle = sums[k][MIDDLE : MIDDLE + 1]
            fa[tok] = two_terms(jnp.exp(middle - sums[k]), heads)
            fb[tok] = two_terms(jnp.exp(sums[k] - middle), heads)
            middles.append(middle)
            afters.append(sums[k][SUB - 1 :] - middle)
            sums[k] = sums[k] + before
            before = sums[k][SUB - 1 :]
            write, read = w_ref[tok], r_ref[tok]
            pairs = jnp.where(upper, dot(write, read, ((1,), (1,))), 0.0).astype(BF16)
            pw[k] = jnp.concatenate([pairs, write], axis=1)
            wt[k] = write.T
            rt[k] = read.T
        into = [middles[0]] + [middles[k] + afters[k - 1] for k in range(1, count)]
        back = [afters[k] + middles[k + 1] for k in range(count - 1)] + [afters[count - 1]]
        between[...] = two_terms(jnp.exp(jnp.concatenate(into + back, axis=0)), heads)
        for k in range(count):
            tok = slice(k * SUB, (k + 1) * SUB)
            fx[tok] = two_terms(jnp.exp(before - sums[k]), heads)
            fg[tok] = two_terms(jnp.exp(sums[k]), heads)
        acc[...] = jnp.zeros_like(acc)

    spread = spread_matrix(heads, head_size, wide, step)
    factor = dot(between[...], spread)
    x1_ref[...] = (x_ref[...].astype(F32) * dot(fx[...], spread)).astype(BF16)
    g1_ref[...] = (g_ref[...].astype(F32) * dot(fg[...], spread)).astype(BF16)
    xs[...] = (x_ref[...].astype(F32) * dot(fa[...], spread)).astype(BF16)
    gs[...] = (g_ref[...].astype(F32) * dot(fb[...], spread)).astype(BF16)
    for k in range(count):
        tok = slice(k * SUB, (k + 1) * SUB)
        took[k] = dot(rt[k], gs[tok])
        wrote[k] = dot(wt[k], xs[tok])

    back = jnp.zeros((state, wide), F32)
    for k in reversed(range(count)):
        back_s[k] = back.astype(BF16)
        if k:
            back = factor[count + k - 1 : count + k] * (back + took[k])
    into = jnp.zeros((state, wide), F32)
    for k in range(count):
        into_s[k] = into.astype(BF16)
        if k + 1 < count:
            into = factor[k + 1 : k + 2] * (into + wrote[k])

    for k in range(count):
        tok = slice(k * SUB, (k + 1) * SUB)
        right = jnp.concatenate([gs[tok], back_s[k]], axis=0)
        left = jnp.concatenate([xs[tok], into_s[k]], axis=0)
        gi_ref[tok] = dot(fa[tok], spread) * dot(pw[k], right)
        acc[k] += dot(left, right, ((1,), (1,)))

    @pl.when(step == pl.num_programs(0) - 1)
    def _():
        for k in range(count):
            tok = slice(k * SUB, (k + 1) * SUB)
            weights = jnp.where(upper, acc[k, :SUB, :SUB], 0.0).astype(BF16)
            out_ref[k, :, :state] = dot(weights, r_ref[tok]) + acc[k, :SUB, SUB:]
            out_ref[k, :, state:] = (dot(wt[k], weights) + acc[k, SUB:, :SUB]).T


def meet_half(place_ref, away, x1_ref, g1_ref, part_hbm, states, out_ref, part, sems, prepare=None):
    state = states.shape[0] // 2
    chips = out_ref.shape[0]
    core = 1 - place_ref[1] if away else place_ref[1]
    blocks = [2 * lax.rem(place_ref[0] + slot, chips) + core for slot in range(chips)]

    def load(slot):
        return pltpu.make_async_copy(part_hbm.at[blocks[slot]], part.at[slot], sems.at[slot])

    for slot in range(chips):
        load(slot).start()
    if prepare:
        prepare()
    for slot in range(chips):
        tok = pl.ds(pl.multiple_of(blocks[slot] * SUB, SUB), SUB)
        to_write = dot(x1_ref[tok], states[state:], ((1,), (1,)))
        to_read = dot(g1_ref[tok], states[:state], ((1,), (1,)))
        load(slot).wait()
        out_ref[slot, :, :state] = part[slot, :, :state] + to_write
        out_ref[slot, :, state:] = part[slot, :, state:] + to_read


def meet_other_kernel(place_ref, x1_ref, g1_ref, part_hbm, st_ref, out_ref, states, part, sems):
    def prepare():
        for p in range(st_ref.shape[0]):
            states[:, p * LANES : (p + 1) * LANES] = st_ref[p].astype(BF16)

    meet_half(place_ref, True, x1_ref, g1_ref, part_hbm, states, out_ref, part, sems, prepare)


def meet_mine_kernel(place_ref, x1_ref, g1_ref, part_hbm, states, out_ref, part, sems):
    meet_half(place_ref, False, x1_ref, g1_ref, part_hbm, states, out_ref, part, sems)


def finish_kernel(gi_ref, st_ref, w_ref, fx, out_hbm, out, sems, *, heads):
    tokens, width = gi_ref.shape
    head_size = width // heads
    state = w_ref.shape[1]
    steps, _, wide = out.shape

    def store(step):
        return pltpu.make_async_copy(out.at[step], out_hbm.at[:, pl.ds(step * wide, wide)], sems.at[step])

    for step in range(steps):
        lanes = slice(step * wide, (step + 1) * wide)
        spread = spread_matrix(heads, head_size, wide, step)
        pairs = range(step * (wide // LANES), (step + 1) * (wide // LANES))
        leaving = jnp.concatenate([st_ref[p, state:].astype(BF16) for p in pairs], axis=1)
        for start in range(0, tokens, WIDE):
            tok = slice(start, start + WIDE)
            out[step, tok] = (gi_ref[tok, lanes] + dot(fx[tok], spread) * dot(w_ref[tok], leaving)).astype(BF16)
        store(step).start()
    for step in range(steps):
        store(step).wait()


def params(mib):
    return pltpu.CompilerParams(vmem_limit_bytes=mib * 2**20)


def in_hbm(array):
    return pltpu.with_memory_space_constraint(array, pltpu.HBM)


HERE = pl.BlockSpec(memory_space=pltpu.VMEM)


def fixed(*shape):
    return pl.BlockSpec(shape, lambda i: (0,) * len(shape))


def summarise(x, g, w, r, ld):
    tokens, width = x.shape
    state = w.shape[1]
    steps = width // FIRST
    there = pl.BlockSpec(memory_space=pltpu.HBM)
    payload = (width // LANES, 2 * state + 8, LANES)
    return pl.pallas_call(
        summary_kernel,
        in_specs=[there] * 5,
        out_specs=there,
        out_shape=jax.ShapeDtypeStruct(payload, F32),
        scratch_shapes=[
            pltpu.VMEM((tokens, LANES), BF16),
            pltpu.VMEM((tokens, LANES), BF16),
            pltpu.VMEM((16, LANES), BF16),
            pltpu.VMEM((state, tokens), BF16),
            pltpu.VMEM((state, tokens), BF16),
            pltpu.VMEM((steps, tokens, FIRST), BF16),
            pltpu.VMEM((steps, tokens, FIRST), BF16),
            pltpu.VMEM((tokens, state), BF16),
            pltpu.VMEM((tokens, state), BF16),
            pltpu.VMEM(ld.shape, F32),
            pltpu.VMEM(payload, F32),
            pltpu.SemaphoreType.DMA((3 * steps + 3,)),
        ],
        compiler_params=params(60),
        name="summary",
    )(x, g, w, r, ld)


def scan_shards(every):
    return pl.pallas_call(
        scan_kernel,
        in_specs=[HERE],
        out_specs=HERE,
        out_shape=jax.ShapeDtypeStruct((every.shape[0], every.shape[1] - 8, LANES), F32),
        compiler_params=params(16),
        name="scan",
    )(every)


def local_gradients(x, g, w, r, ld):
    tokens, width = x.shape
    state = w.shape[1]
    count = tokens // SUB
    wide = pl.BlockSpec((tokens, WIDE), lambda i: (0, i))
    return pl.pallas_call(
        local_kernel,
        grid=(width // WIDE,),
        in_specs=[wide, wide, fixed(tokens, state), fixed(tokens, state), fixed(*ld.shape)],
        out_specs=[wide, fixed(count, SUB, 2 * state), wide, wide, fixed(tokens, LANES)],
        out_shape=[
            pltpu.HBM((tokens, width), F32),
            pltpu.HBM((count, SUB, 2 * state), F32),
            pltpu.HBM((tokens, width), BF16),
            pltpu.HBM((tokens, width), BF16),
            pltpu.HBM((tokens, LANES), BF16),
        ],
        scratch_shapes=[
            pltpu.VMEM((tokens, LANES), BF16),
            pltpu.VMEM((tokens, LANES), BF16),
            pltpu.VMEM((tokens, LANES), BF16),
            pltpu.VMEM((2 * count, LANES), BF16),
            pltpu.VMEM((count, SUB, SUB + state), BF16),
            pltpu.VMEM((count, state, SUB), BF16),
            pltpu.VMEM((count, state, SUB), BF16),
            pltpu.VMEM((tokens, WIDE), BF16),
            pltpu.VMEM((tokens, WIDE), BF16),
            pltpu.VMEM((count, SUB + state, SUB + state), F32),
            pltpu.VMEM((count, state, WIDE), F32),
            pltpu.VMEM((count, state, WIDE), F32),
            pltpu.VMEM((count, state, WIDE), BF16),
            pltpu.VMEM((count, state, WIDE), BF16),
        ],
        compiler_params=params(60),
        cost_estimate=pl.CostEstimate(flops=10**10, bytes_accessed=26 * 10**6, transcendentals=0),
        name="local",
    )(in_hbm(x), in_hbm(g), w, r, ld)


def meet(kernel, place, x1, g1, parts, states, keep):
    tokens, width = x1.shape
    count, _, both = parts.shape
    return pl.pallas_call(
        kernel,
        in_specs=[pl.BlockSpec(memory_space=pltpu.SMEM), HERE, HERE, pl.BlockSpec(memory_space=pltpu.HBM), HERE],
        out_specs=[HERE] * (1 + keep),
        out_shape=[
            jax.ShapeDtypeStruct((count // 2, SUB, both), F32),
            jax.ShapeDtypeStruct((both, width), BF16),
        ][: 1 + keep],
        scratch_shapes=[pltpu.VMEM((count // 2, SUB, both), F32), pltpu.SemaphoreType.DMA((count // 2,))],
        compiler_params=params(16),
        cost_estimate=pl.CostEstimate(flops=10**9, bytes_accessed=4 * 10**6, transcendentals=0),
        name="meet_other" if keep else "meet_mine",
    )(place, x1, g1, in_hbm(parts), states)


def finish(gi, own, w, fx, heads):
    tokens, width = gi.shape
    steps = width // WIDE

    def kernel(*refs):
        finish_kernel(*refs, heads=heads)

    return pl.pallas_call(
        kernel,
        in_specs=[HERE] * 4,
        out_specs=pl.BlockSpec(memory_space=pltpu.HBM),
        out_shape=jax.ShapeDtypeStruct((tokens, width), BF16),
        scratch_shapes=[pltpu.VMEM((steps, tokens, WIDE), BF16), pltpu.SemaphoreType.DMA((steps,))],
        compiler_params=params(16),
        cost_estimate=pl.CostEstimate(flops=2 * 10**9, bytes_accessed=13 * 10**6, transcendentals=0),
        name="finish",
    )(gi, own, w, fx)


def over_chips(terms):
    ranks = lax.axis_size("head")
    arrived = [
        lax.ppermute(terms[d], "head", [(i, (i + 2 * d) % ranks) for i in range(ranks)])
        for d in range(1, terms.shape[0])
    ]
    return sum(arrived, terms[0])


def body(scaled_input, out_grad, write_proj, read_proj, log_decay):
    heads = log_decay.shape[0]
    state = write_proj.shape[1]
    ranks = lax.axis_size("head")
    rank = lax.axis_index("head")
    place = jnp.stack([rank // 2, rank % 2]).astype(jnp.int32)
    every = lax.all_to_all(
        summarise(scaled_input, out_grad, write_proj, read_proj, log_decay), "seq", 0, 0, tiled=True
    )
    local = local_gradients(scaled_input, out_grad, write_proj, read_proj, log_decay)
    every, place, gi, parts, x1, g1, fx = lax.optimization_barrier((every, place, *local))
    own = lax.all_to_all(scan_shards(every), "seq", 0, 0, tiled=True)
    other, states = meet(meet_other_kernel, place, x1, g1, parts, own, True)
    arrived = lax.ppermute(other, "head", [(i, i ^ 1) for i in range(ranks)])
    (mine,) = meet(meet_mine_kernel, place, x1, g1, parts, states, False)
    shared = over_chips(mine + arrived)
    grad_input = finish(gi, own, write_proj, fx, heads)
    return grad_input, shared[:, :state].astype(BF16), shared[:, state:].astype(BF16)


def solution(mesh):
    return jax.shard_map(
        body,
        mesh=mesh,
        in_specs=(
            P("seq", "head"),
            P("seq", "head"),
            P("seq", None),
            P("seq", None),
            P("head", "seq"),
        ),
        out_specs=(P("seq", "head"), P(("seq", "head"), None), P(("seq", "head"), None)),
        check_vma=False,
    )
```

```python
import jax
import jax.numpy as jnp
from jax import lax
from jax.experimental import pallas as pl
from jax.experimental.pallas import tpu as pltpu
from jax.sharding import PartitionSpec as P

SUB = 128
LANES = 128
WIDE = 512
FIRST = 1024
MIDDLE = SUB // 2 - 1
F32 = jnp.float32
BF16 = jnp.bfloat16


def dot(a, b, dims=((1,), (0,))):
    return lax.dot_general(a, b, (dims, ((), ())), preferred_element_type=F32)


def running_sums(decays):
    rows = lax.broadcasted_iota(jnp.int32, (SUB, SUB), 0)
    columns = lax.broadcasted_iota(jnp.int32, (SUB, SUB), 1)
    lower = jnp.where(rows >= columns, 1.0, 0.0).astype(BF16)
    first = decays.astype(BF16)
    left = decays - first.astype(F32)
    second = left.astype(BF16)
    third = (left - second.astype(F32)).astype(BF16)
    sums = []
    for start in range(0, decays.shape[1], SUB):
        tok = slice(start, start + SUB)
        a, b, c = (dot(lower, term[:, tok], ((1,), (1,))) for term in (first, second, third))
        sums.append(a + (b + c))
    return sums


def two_terms(values, heads):
    lane = lax.broadcasted_iota(jnp.int32, values.shape, 1)
    high = values.astype(BF16).astype(F32)
    kept = jnp.where(lane < heads, high, jnp.where(lane < 2 * heads, values - high, 0.0))
    return kept.astype(BF16)


def spread_matrix(heads, head_size, wide, step):
    row = lax.broadcasted_iota(jnp.int32, (LANES, wide), 0)
    column = lax.broadcasted_iota(jnp.int32, (LANES, wide), 1)
    same = lax.rem(row, heads) == (step * wide + column) // head_size
    return jnp.where(same, 1.0, 0.0).astype(BF16)


def summary_kernel(x_hbm, g_hbm, w_hbm, r_hbm, ld_hbm, out_hbm, fx, fg, ends, wt, rt, xb, gb, w_ref, r_ref, ld_ref, out_ref, sems):
    heads, tokens = ld_ref.shape
    steps, _, wide = xb.shape
    head_size = wide * steps // heads
    state = w_ref.shape[1]
    pairs = wide // LANES

    def load(source, target, step, sem):
        columns = pl.ds(pl.multiple_of(step * wide, wide), wide)
        return pltpu.make_async_copy(source.at[:, columns], target.at[step], sems.at[sem])

    def save(step):
        slots = pl.ds(step * pairs, pairs)
        return pltpu.make_async_copy(out_ref.at[slots], out_hbm.at[slots], sems.at[2 * steps + step])

    small = [
        pltpu.make_async_copy(source, target, sems.at[3 * steps + n])
        for n, (source, target) in enumerate(((ld_hbm, ld_ref), (w_hbm, w_ref), (r_hbm, r_ref)))
    ]
    for copy in small:
        copy.start()
    for step in range(steps):
        load(x_hbm, xb, step, step).start()
        load(g_hbm, gb, step, steps + step).start()

    small[0].wait()
    sums = running_sums(jnp.concatenate([ld_ref[...]] * (LANES // heads), axis=0))
    before = jnp.zeros((1, LANES), F32)
    for k in range(len(sums)):
        sums[k] = sums[k] + before
        before = sums[k][SUB - 1 :]
    for k in range(len(sums)):
        tok = slice(k * SUB, (k + 1) * SUB)
        fx[tok] = two_terms(jnp.exp(before - sums[k]), heads)
        fg[tok] = two_terms(jnp.exp(sums[k]), heads)
    ends[...] = two_terms(jnp.exp(jnp.broadcast_to(before, ends.shape)), heads)
    small[1].wait()
    small[2].wait()
    for start in range(0, tokens, SUB):
        tok = slice(start, start + SUB)
        wt[:, tok] = w_ref[tok].T
        rt[:, tok] = r_ref[tok].T

    for step in range(steps):
        spread = spread_matrix(heads, head_size, wide, step)
        load(x_hbm, xb, step, step).wait()
        written = dot(wt[...], (xb[step].astype(F32) * dot(fx[...], spread)).astype(BF16))
        load(g_hbm, gb, step, steps + step).wait()
        collected = dot(rt[...], (gb[step].astype(F32) * dot(fg[...], spread)).astype(BF16))
        decay = dot(ends[...], spread)[:8]
        for pair in range(pairs):
            lanes = slice(pair * LANES, (pair + 1) * LANES)
            out_ref[step * pairs + pair, :state] = written[:, lanes]
            out_ref[step * pairs + pair, state : 2 * state] = collected[:, lanes]
            out_ref[step * pairs + pair, 2 * state :] = decay[:, lanes]
        save(step).start()
    for step in range(steps):
        save(step).wait()


def scan_kernel(in_ref, out_ref):
    shards = in_ref.shape[0]
    state = out_ref.shape[1] // 2
    carried = jnp.zeros((state, LANES), F32)
    for shard in range(shards):
        out_ref[shard, :state] = carried
        carried = in_ref[shard, 2 * state : 2 * state + 1] * carried + in_ref[shard, :state]
    carried = jnp.zeros((state, LANES), F32)
    for shard in reversed(range(shards)):
        out_ref[shard, state:] = carried
        carried = in_ref[shard, 2 * state : 2 * state + 1] * carried + in_ref[shard, state : 2 * state]


def block_of(place_ref, slot, chips, core):
    return 2 * lax.rem(place_ref[0] + slot, chips) + core


def local_kernel(
    place_ref, x_ref, g_ref, w_ref, r_ref, ld_ref, gi_ref, other_ref, mine_ref, x1_ref, g1_ref, fx, fa, fb, fg, between, pw, wt, rt, xs, gs, acc, wrote, took, into_s, back_s
):
    heads, tokens = ld_ref.shape
    wide = x_ref.shape[1]
    head_size = wide * pl.num_programs(0) // heads
    count, state, _ = wt.shape
    step = pl.program_id(0)
    rows = lax.broadcasted_iota(jnp.int32, (SUB, SUB), 0)
    columns = lax.broadcasted_iota(jnp.int32, (SUB, SUB), 1)
    upper = columns >= rows

    @pl.when(step == 0)
    def _():
        sums = running_sums(jnp.concatenate([ld_ref[...]] * (LANES // heads), axis=0))
        before = jnp.zeros((1, LANES), F32)
        middles = []
        afters = []
        for k in range(count):
            tok = slice(k * SUB, (k + 1) * SUB)
            middle = sums[k][MIDDLE : MIDDLE + 1]
            fa[tok] = two_terms(jnp.exp(middle - sums[k]), heads)
            fb[tok] = two_terms(jnp.exp(sums[k] - middle), heads)
            middles.append(middle)
            afters.append(sums[k][SUB - 1 :] - middle)
            sums[k] = sums[k] + before
            before = sums[k][SUB - 1 :]
            write, read = w_ref[tok], r_ref[tok]
            pairs = jnp.where(upper, dot(write, read, ((1,), (1,))), 0.0).astype(BF16)
            pw[k] = jnp.concatenate([pairs, write], axis=1)
            wt[k] = write.T
            rt[k] = read.T
        into = [middles[0]] + [middles[k] + afters[k - 1] for k in range(1, count)]
        back = [afters[k] + middles[k + 1] for k in range(count - 1)] + [afters[count - 1]]
        between[...] = two_terms(jnp.exp(jnp.concatenate(into + back, axis=0)), heads)
        for k in range(count):
            tok = slice(k * SUB, (k + 1) * SUB)
            fx[tok] = two_terms(jnp.exp(before - sums[k]), heads)
            fg[tok] = two_terms(jnp.exp(sums[k]), heads)
        acc[...] = jnp.zeros_like(acc)

    spread = spread_matrix(heads, head_size, wide, step)
    factor = dot(between[...], spread)
    x1_ref[...] = (x_ref[...].astype(F32) * dot(fx[...], spread)).astype(BF16)
    g1_ref[...] = (g_ref[...].astype(F32) * dot(fg[...], spread)).astype(BF16)
    xs[...] = (x_ref[...].astype(F32) * dot(fa[...], spread)).astype(BF16)
    gs[...] = (g_ref[...].astype(F32) * dot(fb[...], spread)).astype(BF16)
    for k in range(count):
        tok = slice(k * SUB, (k + 1) * SUB)
        took[k] = dot(rt[k], gs[tok])
        wrote[k] = dot(wt[k], xs[tok])

    back = jnp.zeros((state, wide), F32)
    for k in reversed(range(count)):
        back_s[k] = back.astype(BF16)
        if k:
            back = factor[count + k - 1 : count + k] * (back + took[k])
    into = jnp.zeros((state, wide), F32)
    for k in range(count):
        into_s[k] = into.astype(BF16)
        if k + 1 < count:
            into = factor[k + 1 : k + 2] * (into + wrote[k])

    for k in range(count):
        tok = slice(k * SUB, (k + 1) * SUB)
        right = jnp.concatenate([gs[tok], back_s[k]], axis=0)
        left = jnp.concatenate([xs[tok], into_s[k]], axis=0)
        gi_ref[tok] = dot(fa[tok], spread) * dot(pw[k], right)
        acc[k] += dot(left, right, ((1,), (1,)))

    @pl.when(step == pl.num_programs(0) - 1)
    def _():
        for out_ref, core in ((other_ref, 1 - place_ref[1]), (mine_ref, place_ref[1])):
            for slot in range(count // 2):
                k = block_of(place_ref, slot, count // 2, core)
                tok = pl.ds(pl.multiple_of(k * SUB, SUB), SUB)
                weights = jnp.where(upper, acc[k, :SUB, :SUB], 0.0).astype(BF16)
                out_ref[slot, :, :state] = dot(weights, r_ref[tok]) + acc[k, :SUB, SUB:]
                out_ref[slot, :, state:] = (dot(wt[k], weights) + acc[k, SUB:, :SUB]).T


def meet_half(place_ref, away, x1_ref, g1_ref, states, out_ref):
    state = states.shape[0] // 2
    chips = out_ref.shape[0]
    core = 1 - place_ref[1] if away else place_ref[1]
    for slot in range(chips):
        tok = pl.ds(pl.multiple_of(block_of(place_ref, slot, chips, core) * SUB, SUB), SUB)
        out_ref[slot, :, :state] = dot(x1_ref[tok], states[state:], ((1,), (1,)))
        out_ref[slot, :, state:] = dot(g1_ref[tok], states[:state], ((1,), (1,)))


def meet_other_kernel(place_ref, x1_ref, g1_ref, st_ref, out_ref, states):
    for p in range(st_ref.shape[0]):
        states[:, p * LANES : (p + 1) * LANES] = st_ref[p].astype(BF16)
    meet_half(place_ref, True, x1_ref, g1_ref, states, out_ref)


def meet_mine_kernel(place_ref, x1_ref, g1_ref, states, out_ref):
    meet_half(place_ref, False, x1_ref, g1_ref, states, out_ref)


def finish_kernel(gi_ref, st_ref, w_ref, fx, out_hbm, out, sems, *, heads):
    tokens, width = gi_ref.shape
    head_size = width // heads
    state = w_ref.shape[1]
    steps, _, wide = out.shape

    def store(step):
        return pltpu.make_async_copy(out.at[step], out_hbm.at[:, pl.ds(step * wide, wide)], sems.at[step])

    for step in range(steps):
        lanes = slice(step * wide, (step + 1) * wide)
        spread = spread_matrix(heads, head_size, wide, step)
        pairs = range(step * (wide // LANES), (step + 1) * (wide // LANES))
        leaving = jnp.concatenate([st_ref[p, state:].astype(BF16) for p in pairs], axis=1)
        for start in range(0, tokens, WIDE):
            tok = slice(start, start + WIDE)
            out[step, tok] = (gi_ref[tok, lanes] + dot(fx[tok], spread) * dot(w_ref[tok], leaving)).astype(BF16)
        store(step).start()
    for step in range(steps):
        store(step).wait()


def params(mib):
    return pltpu.CompilerParams(vmem_limit_bytes=mib * 2**20)


def in_hbm(array):
    return pltpu.with_memory_space_constraint(array, pltpu.HBM)


HERE = pl.BlockSpec(memory_space=pltpu.VMEM)


def fixed(*shape):
    return pl.BlockSpec(shape, lambda i: (0,) * len(shape))


def summarise(x, g, w, r, ld):
    tokens, width = x.shape
    state = w.shape[1]
    steps = width // FIRST
    there = pl.BlockSpec(memory_space=pltpu.HBM)
    payload = (width // LANES, 2 * state + 8, LANES)
    return pl.pallas_call(
        summary_kernel,
        in_specs=[there] * 5,
        out_specs=there,
        out_shape=jax.ShapeDtypeStruct(payload, F32),
        scratch_shapes=[
            pltpu.VMEM((tokens, LANES), BF16),
            pltpu.VMEM((tokens, LANES), BF16),
            pltpu.VMEM((16, LANES), BF16),
            pltpu.VMEM((state, tokens), BF16),
            pltpu.VMEM((state, tokens), BF16),
            pltpu.VMEM((steps, tokens, FIRST), BF16),
            pltpu.VMEM((steps, tokens, FIRST), BF16),
            pltpu.VMEM((tokens, state), BF16),
            pltpu.VMEM((tokens, state), BF16),
            pltpu.VMEM(ld.shape, F32),
            pltpu.VMEM(payload, F32),
            pltpu.SemaphoreType.DMA((3 * steps + 3,)),
        ],
        compiler_params=params(60),
        name="summary",
    )(x, g, w, r, ld)


def scan_shards(every):
    return pl.pallas_call(
        scan_kernel,
        in_specs=[HERE],
        out_specs=HERE,
        out_shape=jax.ShapeDtypeStruct((every.shape[0], every.shape[1] - 8, LANES), F32),
        compiler_params=params(16),
        name="scan",
    )(every)


def local_gradients(place, x, g, w, r, ld):
    tokens, width = x.shape
    state = w.shape[1]
    count = tokens // SUB
    wide = pl.BlockSpec((tokens, WIDE), lambda i: (0, i))
    return pl.pallas_call(
        local_kernel,
        grid=(width // WIDE,),
        in_specs=[pl.BlockSpec(memory_space=pltpu.SMEM), wide, wide, fixed(tokens, state), fixed(tokens, state), fixed(*ld.shape)],
        out_specs=[wide, *[fixed(count // 2, SUB, 2 * state)] * 2, wide, wide, fixed(tokens, LANES)],
        out_shape=[
            pltpu.HBM((tokens, width), F32),
            pltpu.HBM((count // 2, SUB, 2 * state), F32),
            pltpu.HBM((count // 2, SUB, 2 * state), F32),
            pltpu.HBM((tokens, width), BF16),
            pltpu.HBM((tokens, width), BF16),
            pltpu.HBM((tokens, LANES), BF16),
        ],
        scratch_shapes=[
            pltpu.VMEM((tokens, LANES), BF16),
            pltpu.VMEM((tokens, LANES), BF16),
            pltpu.VMEM((tokens, LANES), BF16),
            pltpu.VMEM((2 * count, LANES), BF16),
            pltpu.VMEM((count, SUB, SUB + state), BF16),
            pltpu.VMEM((count, state, SUB), BF16),
            pltpu.VMEM((count, state, SUB), BF16),
            pltpu.VMEM((tokens, WIDE), BF16),
            pltpu.VMEM((tokens, WIDE), BF16),
            pltpu.VMEM((count, SUB + state, SUB + state), F32),
            pltpu.VMEM((count, state, WIDE), F32),
            pltpu.VMEM((count, state, WIDE), F32),
            pltpu.VMEM((count, state, WIDE), BF16),
            pltpu.VMEM((count, state, WIDE), BF16),
        ],
        compiler_params=params(60),
        cost_estimate=pl.CostEstimate(flops=10**10, bytes_accessed=26 * 10**6, transcendentals=0),
        name="local",
    )(place, in_hbm(x), in_hbm(g), w, r, ld)


def meet(kernel, place, x1, g1, states, keep):
    tokens, width = x1.shape
    both = 2 * LANES
    return pl.pallas_call(
        kernel,
        in_specs=[pl.BlockSpec(memory_space=pltpu.SMEM)] + [HERE] * 3,
        out_specs=[HERE] * (1 + keep),
        out_shape=[
            jax.ShapeDtypeStruct((tokens // SUB // 2, SUB, both), F32),
            jax.ShapeDtypeStruct((both, width), BF16),
        ][: 1 + keep],
        compiler_params=params(16),
        cost_estimate=pl.CostEstimate(flops=10**9, bytes_accessed=4 * 10**6, transcendentals=0),
        name="meet_other" if keep else "meet_mine",
    )(place, x1, g1, states)


def finish(gi, own, w, fx, heads):
    tokens, width = gi.shape
    steps = width // WIDE

    def kernel(*refs):
        finish_kernel(*refs, heads=heads)

    return pl.pallas_call(
        kernel,
        in_specs=[HERE] * 4,
        out_specs=pl.BlockSpec(memory_space=pltpu.HBM),
        out_shape=jax.ShapeDtypeStruct((tokens, width), BF16),
        scratch_shapes=[pltpu.VMEM((steps, tokens, WIDE), BF16), pltpu.SemaphoreType.DMA((steps,))],
        compiler_params=params(16),
        cost_estimate=pl.CostEstimate(flops=2 * 10**9, bytes_accessed=13 * 10**6, transcendentals=0),
        name="finish",
    )(gi, own, w, fx)


def over_cores(other):
    ranks = lax.axis_size("head")
    return lax.ppermute(other, "head", [(i, i ^ 1) for i in range(ranks)])


def over_chips(terms, start):
    ranks = lax.axis_size("head")
    arrived = [
        lax.ppermute(terms[d], "head", [(i, (i + 2 * d) % ranks) for i in range(ranks)])
        for d in range(1, terms.shape[0])
    ]
    return sum(arrived, start + terms[0])


def body(scaled_input, out_grad, write_proj, read_proj, log_decay):
    heads = log_decay.shape[0]
    state = write_proj.shape[1]
    rank = lax.axis_index("head")
    place = jnp.stack([rank // 2, rank % 2]).astype(jnp.int32)
    every = lax.all_to_all(
        summarise(scaled_input, out_grad, write_proj, read_proj, log_decay), "seq", 0, 0, tiled=True
    )
    gi, other, mine, x1, g1, fx = local_gradients(
        place, scaled_input, out_grad, write_proj, read_proj, log_decay
    )
    local = over_chips(mine + over_cores(other), 0.0)
    every, place, local, gi, x1, g1, fx = lax.optimization_barrier((every, place, local, gi, x1, g1, fx))
    own = lax.all_to_all(scan_shards(every), "seq", 0, 0, tiled=True)
    other, states = meet(meet_other_kernel, place, x1, g1, own, True)
    arrived = over_cores(other)
    (mine,) = meet(meet_mine_kernel, place, x1, g1, states, False)
    shared = over_chips(mine + arrived, local)
    grad_input = finish(gi, own, write_proj, fx, heads)
    return grad_input, shared[:, :state].astype(BF16), shared[:, state:].astype(BF16)


def solution(mesh):
    return jax.shard_map(
        body,
        mesh=mesh,
        in_specs=(
            P("seq", "head"),
            P("seq", "head"),
            P("seq", None),
            P("seq", None),
            P("head", "seq"),
        ),
        out_specs=(P("seq", "head"), P(("seq", "head"), None), P(("seq", "head"), None)),
        check_vma=False,
    )
```

```python
import jax
import jax.numpy as jnp
from jax import lax
from jax.experimental import pallas as pl
from jax.experimental.pallas import tpu as pltpu
from jax.sharding import PartitionSpec as P

SUB = 128
LANES = 128
WIDE = 512
FIRST = 1024
MIDDLE = SUB // 2 - 1
F32 = jnp.float32
BF16 = jnp.bfloat16


def dot(a, b, dims=((1,), (0,))):
    return lax.dot_general(a, b, (dims, ((), ())), preferred_element_type=F32)


def running_sums(decays):
    rows = lax.broadcasted_iota(jnp.int32, (SUB, SUB), 0)
    columns = lax.broadcasted_iota(jnp.int32, (SUB, SUB), 1)
    lower = jnp.where(rows >= columns, 1.0, 0.0).astype(BF16)
    first = decays.astype(BF16)
    left = decays - first.astype(F32)
    second = left.astype(BF16)
    third = (left - second.astype(F32)).astype(BF16)
    sums = []
    for start in range(0, decays.shape[1], SUB):
        tok = slice(start, start + SUB)
        a, b, c = (dot(lower, term[:, tok], ((1,), (1,))) for term in (first, second, third))
        sums.append(a + (b + c))
    return sums


def two_terms(values, heads):
    lane = lax.broadcasted_iota(jnp.int32, values.shape, 1)
    high = values.astype(BF16).astype(F32)
    kept = jnp.where(lane < heads, high, jnp.where(lane < 2 * heads, values - high, 0.0))
    return kept.astype(BF16)


def spread_matrix(heads, head_size, wide, step):
    row = lax.broadcasted_iota(jnp.int32, (LANES, wide), 0)
    column = lax.broadcasted_iota(jnp.int32, (LANES, wide), 1)
    same = lax.rem(row, heads) == (step * wide + column) // head_size
    return jnp.where(same, 1.0, 0.0).astype(BF16)


def summary_kernel(x_hbm, g_hbm, w_hbm, r_hbm, ld_hbm, out_hbm, fx, fg, ends, wt, rt, xb, gb, w_ref, r_ref, ld_ref, out_ref, sems):
    heads, tokens = ld_ref.shape
    steps, _, wide = xb.shape
    head_size = wide * steps // heads
    state = w_ref.shape[1]
    pairs = wide // LANES

    def load(source, target, step, sem):
        columns = pl.ds(pl.multiple_of(step * wide, wide), wide)
        return pltpu.make_async_copy(source.at[:, columns], target.at[step], sems.at[sem])

    def save(step):
        slots = pl.ds(step * pairs, pairs)
        return pltpu.make_async_copy(out_ref.at[slots], out_hbm.at[slots], sems.at[2 * steps + step])

    small = [
        pltpu.make_async_copy(source, target, sems.at[3 * steps + n])
        for n, (source, target) in enumerate(((ld_hbm, ld_ref), (w_hbm, w_ref), (r_hbm, r_ref)))
    ]
    for copy in small:
        copy.start()
    for step in range(steps):
        load(x_hbm, xb, step, step).start()
        load(g_hbm, gb, step, steps + step).start()

    small[0].wait()
    sums = running_sums(jnp.concatenate([ld_ref[...]] * (LANES // heads), axis=0))
    before = jnp.zeros((1, LANES), F32)
    for k in range(len(sums)):
        sums[k] = sums[k] + before
        before = sums[k][SUB - 1 :]
    for k in range(len(sums)):
        tok = slice(k * SUB, (k + 1) * SUB)
        fx[tok] = two_terms(jnp.exp(before - sums[k]), heads)
        fg[tok] = two_terms(jnp.exp(sums[k]), heads)
    ends[...] = two_terms(jnp.exp(jnp.broadcast_to(before, ends.shape)), heads)
    small[1].wait()
    small[2].wait()
    for start in range(0, tokens, SUB):
        tok = slice(start, start + SUB)
        wt[:, tok] = w_ref[tok].T
        rt[:, tok] = r_ref[tok].T

    for step in range(steps):
        spread = spread_matrix(heads, head_size, wide, step)
        load(x_hbm, xb, step, step).wait()
        written = dot(wt[...], (xb[step].astype(F32) * dot(fx[...], spread)).astype(BF16))
        load(g_hbm, gb, step, steps + step).wait()
        collected = dot(rt[...], (gb[step].astype(F32) * dot(fg[...], spread)).astype(BF16))
        decay = dot(ends[...], spread)[:8]
        for pair in range(pairs):
            lanes = slice(pair * LANES, (pair + 1) * LANES)
            out_ref[step * pairs + pair, :state] = written[:, lanes]
            out_ref[step * pairs + pair, state : 2 * state] = collected[:, lanes]
            out_ref[step * pairs + pair, 2 * state :] = decay[:, lanes]
        save(step).start()
    for step in range(steps):
        save(step).wait()


def scan_kernel(in_ref, out_ref):
    shards = in_ref.shape[0]
    state = out_ref.shape[1] // 2
    carried = jnp.zeros((state, LANES), F32)
    for shard in range(shards):
        out_ref[shard, :state] = carried
        carried = in_ref[shard, 2 * state : 2 * state + 1] * carried + in_ref[shard, :state]
    carried = jnp.zeros((state, LANES), F32)
    for shard in reversed(range(shards)):
        out_ref[shard, state:] = carried
        carried = in_ref[shard, 2 * state : 2 * state + 1] * carried + in_ref[shard, state : 2 * state]


def block_of(place_ref, slot, chips, core):
    return 2 * lax.rem(place_ref[0] + slot, chips) + core


def local_kernel(
    place_ref, x_ref, g_ref, w_ref, r_ref, ld_ref, gi_ref, other_ref, mine_ref, x1_ref, g1_ref, fx, fa, fb, fg, between, pw, wt, rt, xs, gs, acc, wrote, took, into_s, back_s
):
    heads, tokens = ld_ref.shape
    wide = x_ref.shape[1]
    head_size = wide * pl.num_programs(0) // heads
    count, state, _ = wt.shape
    step = pl.program_id(0)
    rows = lax.broadcasted_iota(jnp.int32, (SUB, SUB), 0)
    columns = lax.broadcasted_iota(jnp.int32, (SUB, SUB), 1)
    upper = columns >= rows

    @pl.when(step == 0)
    def _():
        sums = running_sums(jnp.concatenate([ld_ref[...]] * (LANES // heads), axis=0))
        before = jnp.zeros((1, LANES), F32)
        middles = []
        afters = []
        for k in range(count):
            tok = slice(k * SUB, (k + 1) * SUB)
            middle = sums[k][MIDDLE : MIDDLE + 1]
            fa[tok] = two_terms(jnp.exp(middle - sums[k]), heads)
            fb[tok] = two_terms(jnp.exp(sums[k] - middle), heads)
            middles.append(middle)
            afters.append(sums[k][SUB - 1 :] - middle)
            sums[k] = sums[k] + before
            before = sums[k][SUB - 1 :]
            write, read = w_ref[tok], r_ref[tok]
            pairs = jnp.where(upper, dot(write, read, ((1,), (1,))), 0.0).astype(BF16)
            pw[k] = jnp.concatenate([pairs, write], axis=1)
            wt[k] = write.T
            rt[k] = read.T
        into = [middles[0]] + [middles[k] + afters[k - 1] for k in range(1, count)]
        back = [afters[k] + middles[k + 1] for k in range(count - 1)] + [afters[count - 1]]
        between[...] = two_terms(jnp.exp(jnp.concatenate(into + back, axis=0)), heads)
        for k in range(count):
            tok = slice(k * SUB, (k + 1) * SUB)
            fx[tok] = two_terms(jnp.exp(before - sums[k]), heads)
            fg[tok] = two_terms(jnp.exp(sums[k]), heads)
        acc[...] = jnp.zeros_like(acc)

    spread = spread_matrix(heads, head_size, wide, step)
    factor = dot(between[...], spread)
    x1_ref[...] = (x_ref[...].astype(F32) * dot(fx[...], spread)).astype(BF16)
    g1_ref[...] = (g_ref[...].astype(F32) * dot(fg[...], spread)).astype(BF16)
    xs[...] = (x_ref[...].astype(F32) * dot(fa[...], spread)).astype(BF16)
    gs[...] = (g_ref[...].astype(F32) * dot(fb[...], spread)).astype(BF16)
    for k in range(count):
        tok = slice(k * SUB, (k + 1) * SUB)
        took[k] = dot(rt[k], gs[tok])
        wrote[k] = dot(wt[k], xs[tok])

    back = jnp.zeros((state, wide), F32)
    for k in reversed(range(count)):
        back_s[k] = back.astype(BF16)
        if k:
            back = factor[count + k - 1 : count + k] * (back + took[k])
    into = jnp.zeros((state, wide), F32)
    for k in range(count):
        into_s[k] = into.astype(BF16)
        if k + 1 < count:
            into = factor[k + 1 : k + 2] * (into + wrote[k])

    for k in range(count):
        tok = slice(k * SUB, (k + 1) * SUB)
        right = jnp.concatenate([gs[tok], back_s[k]], axis=0)
        left = jnp.concatenate([xs[tok], into_s[k]], axis=0)
        gi_ref[tok] = dot(fa[tok], spread) * dot(pw[k], right)
        acc[k] += dot(left, right, ((1,), (1,)))

    @pl.when(step == pl.num_programs(0) - 1)
    def _():
        for out_ref, core in ((other_ref, 1 - place_ref[1]), (mine_ref, place_ref[1])):
            for slot in range(count // 2):
                k = block_of(place_ref, slot, count // 2, core)
                tok = pl.ds(pl.multiple_of(k * SUB, SUB), SUB)
                weights = jnp.where(upper, acc[k, :SUB, :SUB], 0.0).astype(BF16)
                out_ref[slot, :, :state] = dot(weights, r_ref[tok]) + acc[k, :SUB, SUB:]
                out_ref[slot, :, state:] = (dot(wt[k], weights) + acc[k, SUB:, :SUB]).T


def meet_half(place_ref, away, x1_ref, g1_ref, states, out_ref):
    state = states.shape[0] // 2
    chips = out_ref.shape[0]
    core = 1 - place_ref[1] if away else place_ref[1]
    for slot in range(chips):
        tok = pl.ds(pl.multiple_of(block_of(place_ref, slot, chips, core) * SUB, SUB), SUB)
        out_ref[slot, :, :state] = dot(x1_ref[tok], states[state:], ((1,), (1,)))
        out_ref[slot, :, state:] = dot(g1_ref[tok], states[:state], ((1,), (1,)))


def meet_other_kernel(place_ref, x1_ref, g1_ref, st_ref, out_ref, states):
    for p in range(st_ref.shape[0]):
        states[:, p * LANES : (p + 1) * LANES] = st_ref[p].astype(BF16)
    meet_half(place_ref, True, x1_ref, g1_ref, states, out_ref)


def meet_mine_kernel(place_ref, x1_ref, g1_ref, states, out_ref):
    meet_half(place_ref, False, x1_ref, g1_ref, states, out_ref)


def finish_kernel(gi_ref, st_ref, w_ref, fx, out_hbm, out, sems, *, heads):
    tokens, width = gi_ref.shape
    head_size = width // heads
    state = w_ref.shape[1]
    steps, _, wide = out.shape

    def store(step):
        return pltpu.make_async_copy(out.at[step], out_hbm.at[:, pl.ds(step * wide, wide)], sems.at[step])

    for step in range(steps):
        lanes = slice(step * wide, (step + 1) * wide)
        spread = spread_matrix(heads, head_size, wide, step)
        pairs = range(step * (wide // LANES), (step + 1) * (wide // LANES))
        leaving = jnp.concatenate([st_ref[p, state:].astype(BF16) for p in pairs], axis=1)
        for start in range(0, tokens, WIDE):
            tok = slice(start, start + WIDE)
            out[step, tok] = (gi_ref[tok, lanes] + dot(fx[tok], spread) * dot(w_ref[tok], leaving)).astype(BF16)
        store(step).start()
    for step in range(steps):
        store(step).wait()


def params(mib):
    return pltpu.CompilerParams(vmem_limit_bytes=mib * 2**20)


def in_hbm(array):
    return pltpu.with_memory_space_constraint(array, pltpu.HBM)


HERE = pl.BlockSpec(memory_space=pltpu.VMEM)


def fixed(*shape):
    return pl.BlockSpec(shape, lambda i: (0,) * len(shape))


def summarise(x, g, w, r, ld):
    tokens, width = x.shape
    state = w.shape[1]
    steps = width // FIRST
    there = pl.BlockSpec(memory_space=pltpu.HBM)
    payload = (width // LANES, 2 * state + 8, LANES)
    return pl.pallas_call(
        summary_kernel,
        in_specs=[there] * 5,
        out_specs=there,
        out_shape=jax.ShapeDtypeStruct(payload, F32),
        scratch_shapes=[
            pltpu.VMEM((tokens, LANES), BF16),
            pltpu.VMEM((tokens, LANES), BF16),
            pltpu.VMEM((16, LANES), BF16),
            pltpu.VMEM((state, tokens), BF16),
            pltpu.VMEM((state, tokens), BF16),
            pltpu.VMEM((steps, tokens, FIRST), BF16),
            pltpu.VMEM((steps, tokens, FIRST), BF16),
            pltpu.VMEM((tokens, state), BF16),
            pltpu.VMEM((tokens, state), BF16),
            pltpu.VMEM(ld.shape, F32),
            pltpu.VMEM(payload, F32),
            pltpu.SemaphoreType.DMA((3 * steps + 3,)),
        ],
        compiler_params=params(60),
        name="summary",
    )(x, g, w, r, ld)


def scan_shards(every):
    return pl.pallas_call(
        scan_kernel,
        in_specs=[HERE],
        out_specs=HERE,
        out_shape=jax.ShapeDtypeStruct((every.shape[0], every.shape[1] - 8, LANES), F32),
        compiler_params=params(16),
        name="scan",
    )(every)


def local_gradients(place, x, g, w, r, ld):
    tokens, width = x.shape
    state = w.shape[1]
    count = tokens // SUB
    wide = pl.BlockSpec((tokens, WIDE), lambda i: (0, i))
    return pl.pallas_call(
        local_kernel,
        grid=(width // WIDE,),
        in_specs=[pl.BlockSpec(memory_space=pltpu.SMEM), wide, wide, fixed(tokens, state), fixed(tokens, state), fixed(*ld.shape)],
        out_specs=[wide, *[fixed(count // 2, SUB, 2 * state)] * 2, wide, wide, fixed(tokens, LANES)],
        out_shape=[
            pltpu.HBM((tokens, width), F32),
            pltpu.HBM((count // 2, SUB, 2 * state), F32),
            pltpu.HBM((count // 2, SUB, 2 * state), F32),
            pltpu.HBM((tokens, width), BF16),
            pltpu.HBM((tokens, width), BF16),
            pltpu.HBM((tokens, LANES), BF16),
        ],
        scratch_shapes=[
            pltpu.VMEM((tokens, LANES), BF16),
            pltpu.VMEM((tokens, LANES), BF16),
            pltpu.VMEM((tokens, LANES), BF16),
            pltpu.VMEM((2 * count, LANES), BF16),
            pltpu.VMEM((count, SUB, SUB + state), BF16),
            pltpu.VMEM((count, state, SUB), BF16),
            pltpu.VMEM((count, state, SUB), BF16),
            pltpu.VMEM((tokens, WIDE), BF16),
            pltpu.VMEM((tokens, WIDE), BF16),
            pltpu.VMEM((count, SUB + state, SUB + state), F32),
            pltpu.VMEM((count, state, WIDE), F32),
            pltpu.VMEM((count, state, WIDE), F32),
            pltpu.VMEM((count, state, WIDE), BF16),
            pltpu.VMEM((count, state, WIDE), BF16),
        ],
        compiler_params=params(60),
        cost_estimate=pl.CostEstimate(flops=10**10, bytes_accessed=26 * 10**6, transcendentals=0),
        name="local",
    )(place, in_hbm(x), in_hbm(g), w, r, ld)


def meet(kernel, place, x1, g1, states, keep):
    tokens, width = x1.shape
    both = 2 * LANES
    return pl.pallas_call(
        kernel,
        in_specs=[pl.BlockSpec(memory_space=pltpu.SMEM)] + [HERE] * 3,
        out_specs=[HERE] * (1 + keep),
        out_shape=[
            jax.ShapeDtypeStruct((tokens // SUB // 2, SUB, both), F32),
            jax.ShapeDtypeStruct((both, width), BF16),
        ][: 1 + keep],
        compiler_params=params(16),
        cost_estimate=pl.CostEstimate(flops=10**9, bytes_accessed=4 * 10**6, transcendentals=0),
        name="meet_other" if keep else "meet_mine",
    )(place, x1, g1, states)


def finish(gi, own, w, fx, heads):
    tokens, width = gi.shape
    steps = width // WIDE

    def kernel(*refs):
        finish_kernel(*refs, heads=heads)

    return pl.pallas_call(
        kernel,
        in_specs=[HERE] * 4,
        out_specs=pl.BlockSpec(memory_space=pltpu.HBM),
        out_shape=jax.ShapeDtypeStruct((tokens, width), BF16),
        scratch_shapes=[pltpu.VMEM((steps, tokens, WIDE), BF16), pltpu.SemaphoreType.DMA((steps,))],
        compiler_params=params(16),
        cost_estimate=pl.CostEstimate(flops=2 * 10**9, bytes_accessed=13 * 10**6, transcendentals=0),
        name="finish",
    )(gi, own, w, fx)


def over_cores(other):
    ranks = lax.axis_size("head")
    return lax.ppermute(other, "head", [(i, i ^ 1) for i in range(ranks)])


def over_chips(terms):
    ranks = lax.axis_size("head")
    arrived = [
        lax.ppermute(terms[d], "head", [(i, (i + 2 * d) % ranks) for i in range(ranks)])
        for d in range(1, terms.shape[0])
    ]
    return sum(arrived, terms[0])


def body(scaled_input, out_grad, write_proj, read_proj, log_decay):
    heads = log_decay.shape[0]
    state = write_proj.shape[1]
    rank = lax.axis_index("head")
    place = jnp.stack([rank // 2, rank % 2]).astype(jnp.int32)
    every = lax.all_to_all(
        summarise(scaled_input, out_grad, write_proj, read_proj, log_decay), "seq", 0, 0, tiled=True
    )
    gi, other, mine, x1, g1, fx = local_gradients(
        place, scaled_input, out_grad, write_proj, read_proj, log_decay
    )
    local = mine + over_cores(other)
    every, place, local, gi, x1, g1, fx = lax.optimization_barrier((every, place, local, gi, x1, g1, fx))
    own = lax.all_to_all(scan_shards(every), "seq", 0, 0, tiled=True)
    other, states = meet(meet_other_kernel, place, x1, g1, own, True)
    arrived = over_cores(other)
    (mine,) = meet(meet_mine_kernel, place, x1, g1, states, False)
    shared = over_chips(mine + arrived + local)
    grad_input = finish(gi, own, write_proj, fx, heads)
    return grad_input, shared[:, :state].astype(BF16), shared[:, state:].astype(BF16)


def solution(mesh):
    return jax.shard_map(
        body,
        mesh=mesh,
        in_specs=(
            P("seq", "head"),
            P("seq", "head"),
            P("seq", None),
            P("seq", None),
            P("head", "seq"),
        ),
        out_specs=(P("seq", "head"), P(("seq", "head"), None), P(("seq", "head"), None)),
        check_vma=False,
    )
```

```python
import jax
import jax.numpy as jnp
from jax import lax
from jax.experimental import pallas as pl
from jax.experimental.pallas import tpu as pltpu
from jax.sharding import PartitionSpec as P

SUB = 128
LANES = 128
WIDE = 512
FIRST = 1024
MIDDLE = SUB // 2 - 1
F32 = jnp.float32
BF16 = jnp.bfloat16


def dot(a, b, dims=((1,), (0,))):
    return lax.dot_general(a, b, (dims, ((), ())), preferred_element_type=F32)


def running_sums(decays):
    rows = lax.broadcasted_iota(jnp.int32, (SUB, SUB), 0)
    columns = lax.broadcasted_iota(jnp.int32, (SUB, SUB), 1)
    lower = jnp.where(rows >= columns, 1.0, 0.0).astype(BF16)
    first = decays.astype(BF16)
    left = decays - first.astype(F32)
    second = left.astype(BF16)
    third = (left - second.astype(F32)).astype(BF16)
    sums = []
    for start in range(0, decays.shape[1], SUB):
        tok = slice(start, start + SUB)
        a, b, c = (dot(lower, term[:, tok], ((1,), (1,))) for term in (first, second, third))
        sums.append(a + (b + c))
    return sums


def two_terms(values, heads):
    lane = lax.broadcasted_iota(jnp.int32, values.shape, 1)
    high = values.astype(BF16).astype(F32)
    kept = jnp.where(lane < heads, high, jnp.where(lane < 2 * heads, values - high, 0.0))
    return kept.astype(BF16)


def spread_matrix(heads, head_size, wide, step):
    row = lax.broadcasted_iota(jnp.int32, (LANES, wide), 0)
    column = lax.broadcasted_iota(jnp.int32, (LANES, wide), 1)
    same = lax.rem(row, heads) == (step * wide + column) // head_size
    return jnp.where(same, 1.0, 0.0).astype(BF16)


def summary_kernel(x_hbm, g_hbm, w_hbm, r_hbm, ld_hbm, out_hbm, fx, fg, ends, wt, rt, xb, gb, w_ref, r_ref, ld_ref, out_ref, sems):
    heads, tokens = ld_ref.shape
    steps, _, wide = xb.shape
    head_size = wide * steps // heads
    state = w_ref.shape[1]
    pairs = wide // LANES

    def load(source, target, step, sem):
        columns = pl.ds(pl.multiple_of(step * wide, wide), wide)
        return pltpu.make_async_copy(source.at[:, columns], target.at[step], sems.at[sem])

    def save(step):
        slots = pl.ds(step * pairs, pairs)
        return pltpu.make_async_copy(out_ref.at[slots], out_hbm.at[slots], sems.at[2 * steps + step])

    small = [
        pltpu.make_async_copy(source, target, sems.at[3 * steps + n])
        for n, (source, target) in enumerate(((ld_hbm, ld_ref), (w_hbm, w_ref), (r_hbm, r_ref)))
    ]
    for copy in small:
        copy.start()
    for step in range(steps):
        load(x_hbm, xb, step, step).start()
        load(g_hbm, gb, step, steps + step).start()

    small[0].wait()
    sums = running_sums(jnp.concatenate([ld_ref[...]] * (LANES // heads), axis=0))
    before = jnp.zeros((1, LANES), F32)
    for k in range(len(sums)):
        sums[k] = sums[k] + before
        before = sums[k][SUB - 1 :]
    for k in range(len(sums)):
        tok = slice(k * SUB, (k + 1) * SUB)
        fx[tok] = two_terms(jnp.exp(before - sums[k]), heads)
        fg[tok] = two_terms(jnp.exp(sums[k]), heads)
    ends[...] = two_terms(jnp.exp(jnp.broadcast_to(before, ends.shape)), heads)
    small[1].wait()
    small[2].wait()
    for start in range(0, tokens, SUB):
        tok = slice(start, start + SUB)
        wt[:, tok] = w_ref[tok].T
        rt[:, tok] = r_ref[tok].T

    for step in range(steps):
        spread = spread_matrix(heads, head_size, wide, step)
        load(x_hbm, xb, step, step).wait()
        written = dot(wt[...], (xb[step].astype(F32) * dot(fx[...], spread)).astype(BF16))
        load(g_hbm, gb, step, steps + step).wait()
        collected = dot(rt[...], (gb[step].astype(F32) * dot(fg[...], spread)).astype(BF16))
        decay = dot(ends[...], spread)[:8]
        for pair in range(pairs):
            lanes = slice(pair * LANES, (pair + 1) * LANES)
            out_ref[step * pairs + pair, :state] = written[:, lanes]
            out_ref[step * pairs + pair, state : 2 * state] = collected[:, lanes]
            out_ref[step * pairs + pair, 2 * state :] = decay[:, lanes]
        save(step).start()
    for step in range(steps):
        save(step).wait()


def scan_kernel(in_ref, out_ref):
    shards = in_ref.shape[0]
    state = out_ref.shape[1] // 2
    carried = jnp.zeros((state, LANES), F32)
    for shard in range(shards):
        out_ref[shard, :state] = carried
        carried = in_ref[shard, 2 * state : 2 * state + 1] * carried + in_ref[shard, :state]
    carried = jnp.zeros((state, LANES), F32)
    for shard in reversed(range(shards)):
        out_ref[shard, state:] = carried
        carried = in_ref[shard, 2 * state : 2 * state + 1] * carried + in_ref[shard, state : 2 * state]


def block_of(place_ref, slot, chips, core):
    return 2 * lax.rem(place_ref[0] + slot, chips) + core


def local_kernel(
    place_ref, x_ref, g_ref, w_ref, r_ref, ld_ref, gi_ref, other_ref, mine_ref, x1_ref, g1_ref, fx, fa, fb, fg, between, pw, wt, rt, xs, gs, acc, wrote, took, into_s, back_s
):
    heads, tokens = ld_ref.shape
    wide = x_ref.shape[1]
    head_size = wide * pl.num_programs(0) // heads
    count, state, _ = wt.shape
    step = pl.program_id(0)
    rows = lax.broadcasted_iota(jnp.int32, (SUB, SUB), 0)
    columns = lax.broadcasted_iota(jnp.int32, (SUB, SUB), 1)
    upper = columns >= rows

    @pl.when(step == 0)
    def _():
        sums = running_sums(jnp.concatenate([ld_ref[...]] * (LANES // heads), axis=0))
        before = jnp.zeros((1, LANES), F32)
        middles = []
        afters = []
        for k in range(count):
            tok = slice(k * SUB, (k + 1) * SUB)
            middle = sums[k][MIDDLE : MIDDLE + 1]
            fa[tok] = two_terms(jnp.exp(middle - sums[k]), heads)
            fb[tok] = two_terms(jnp.exp(sums[k] - middle), heads)
            middles.append(middle)
            afters.append(sums[k][SUB - 1 :] - middle)
            sums[k] = sums[k] + before
            before = sums[k][SUB - 1 :]
            write, read = w_ref[tok], r_ref[tok]
            pairs = jnp.where(upper, dot(write, read, ((1,), (1,))), 0.0).astype(BF16)
            pw[k] = jnp.concatenate([pairs, write], axis=1)
            wt[k] = write.T
            rt[k] = read.T
        into = [middles[0]] + [middles[k] + afters[k - 1] for k in range(1, count)]
        back = [afters[k] + middles[k + 1] for k in range(count - 1)] + [afters[count - 1]]
        between[...] = two_terms(jnp.exp(jnp.concatenate(into + back, axis=0)), heads)
        for k in range(count):
            tok = slice(k * SUB, (k + 1) * SUB)
            fx[tok] = two_terms(jnp.exp(before - sums[k]), heads)
            fg[tok] = two_terms(jnp.exp(sums[k]), heads)
        acc[...] = jnp.zeros_like(acc)

    spread = spread_matrix(heads, head_size, wide, step)
    factor = dot(between[...], spread)
    x1_ref[...] = (x_ref[...].astype(F32) * dot(fx[...], spread)).astype(BF16)
    g1_ref[...] = (g_ref[...].astype(F32) * dot(fg[...], spread)).astype(BF16)
    xs[...] = (x_ref[...].astype(F32) * dot(fa[...], spread)).astype(BF16)
    gs[...] = (g_ref[...].astype(F32) * dot(fb[...], spread)).astype(BF16)
    for k in range(count):
        tok = slice(k * SUB, (k + 1) * SUB)
        took[k] = dot(rt[k], gs[tok])
        wrote[k] = dot(wt[k], xs[tok])

    back = jnp.zeros((state, wide), F32)
    for k in reversed(range(count)):
        back_s[k] = back.astype(BF16)
        if k:
            back = factor[count + k - 1 : count + k] * (back + took[k])
    into = jnp.zeros((state, wide), F32)
    for k in range(count):
        into_s[k] = into.astype(BF16)
        if k + 1 < count:
            into = factor[k + 1 : k + 2] * (into + wrote[k])

    for k in range(count):
        tok = slice(k * SUB, (k + 1) * SUB)
        right = jnp.concatenate([gs[tok], back_s[k]], axis=0)
        left = jnp.concatenate([xs[tok], into_s[k]], axis=0)
        gi_ref[tok] = dot(fa[tok], spread) * dot(pw[k], right)
        acc[k] += dot(left, right, ((1,), (1,)))

    @pl.when(step == pl.num_programs(0) - 1)
    def _():
        for out_ref, core in ((other_ref, 1 - place_ref[1]), (mine_ref, place_ref[1])):
            for slot in range(count // 2):
                k = block_of(place_ref, slot, count // 2, core)
                tok = pl.ds(pl.multiple_of(k * SUB, SUB), SUB)
                weights = jnp.where(upper, acc[k, :SUB, :SUB], 0.0).astype(BF16)
                out_ref[slot, :, :state] = dot(weights, r_ref[tok]) + acc[k, :SUB, SUB:]
                out_ref[slot, :, state:] = (dot(wt[k], weights) + acc[k, SUB:, :SUB]).T


def meet_half(place_ref, away, x1_ref, g1_ref, states, out_ref):
    state = states.shape[0] // 2
    chips = out_ref.shape[0]
    core = 1 - place_ref[1] if away else place_ref[1]
    for slot in range(chips):
        tok = pl.ds(pl.multiple_of(block_of(place_ref, slot, chips, core) * SUB, SUB), SUB)
        out_ref[slot, :, :state] = dot(x1_ref[tok], states[state:], ((1,), (1,)))
        out_ref[slot, :, state:] = dot(g1_ref[tok], states[:state], ((1,), (1,)))


def meet_other_kernel(place_ref, x1_ref, g1_ref, st_ref, out_ref, states):
    for p in range(st_ref.shape[0]):
        states[:, p * LANES : (p + 1) * LANES] = st_ref[p].astype(BF16)
    meet_half(place_ref, True, x1_ref, g1_ref, states, out_ref)


def meet_mine_kernel(place_ref, x1_ref, g1_ref, states, out_ref):
    meet_half(place_ref, False, x1_ref, g1_ref, states, out_ref)


def finish_kernel(gi_ref, st_ref, w_ref, fx, out_hbm, out, sems, *, heads):
    tokens, width = gi_ref.shape
    head_size = width // heads
    state = w_ref.shape[1]
    steps, _, wide = out.shape

    def store(step):
        return pltpu.make_async_copy(out.at[step], out_hbm.at[:, pl.ds(step * wide, wide)], sems.at[step])

    for step in range(steps):
        lanes = slice(step * wide, (step + 1) * wide)
        spread = spread_matrix(heads, head_size, wide, step)
        pairs = range(step * (wide // LANES), (step + 1) * (wide // LANES))
        leaving = jnp.concatenate([st_ref[p, state:].astype(BF16) for p in pairs], axis=1)
        for start in range(0, tokens, WIDE):
            tok = slice(start, start + WIDE)
            out[step, tok] = (gi_ref[tok, lanes] + dot(fx[tok], spread) * dot(w_ref[tok], leaving)).astype(BF16)
        store(step).start()
    for step in range(steps):
        store(step).wait()


def params(mib):
    return pltpu.CompilerParams(vmem_limit_bytes=mib * 2**20)


def in_hbm(array):
    return pltpu.with_memory_space_constraint(array, pltpu.HBM)


HERE = pl.BlockSpec(memory_space=pltpu.VMEM)


def fixed(*shape):
    return pl.BlockSpec(shape, lambda i: (0,) * len(shape))


def summarise(x, g, w, r, ld):
    tokens, width = x.shape
    state = w.shape[1]
    steps = width // FIRST
    there = pl.BlockSpec(memory_space=pltpu.HBM)
    payload = (width // LANES, 2 * state + 8, LANES)
    return pl.pallas_call(
        summary_kernel,
        in_specs=[there] * 5,
        out_specs=there,
        out_shape=jax.ShapeDtypeStruct(payload, F32),
        scratch_shapes=[
            pltpu.VMEM((tokens, LANES), BF16),
            pltpu.VMEM((tokens, LANES), BF16),
            pltpu.VMEM((16, LANES), BF16),
            pltpu.VMEM((state, tokens), BF16),
            pltpu.VMEM((state, tokens), BF16),
            pltpu.VMEM((steps, tokens, FIRST), BF16),
            pltpu.VMEM((steps, tokens, FIRST), BF16),
            pltpu.VMEM((tokens, state), BF16),
            pltpu.VMEM((tokens, state), BF16),
            pltpu.VMEM(ld.shape, F32),
            pltpu.VMEM(payload, F32),
            pltpu.SemaphoreType.DMA((3 * steps + 3,)),
        ],
        compiler_params=params(60),
        name="summary",
    )(x, g, w, r, ld)


def scan_shards(every):
    return pl.pallas_call(
        scan_kernel,
        in_specs=[HERE],
        out_specs=HERE,
        out_shape=jax.ShapeDtypeStruct((every.shape[0], every.shape[1] - 8, LANES), F32),
        compiler_params=params(16),
        name="scan",
    )(every)


def local_gradients(place, x, g, w, r, ld):
    tokens, width = x.shape
    state = w.shape[1]
    count = tokens // SUB
    wide = pl.BlockSpec((tokens, WIDE), lambda i: (0, i))
    return pl.pallas_call(
        local_kernel,
        grid=(width // WIDE,),
        in_specs=[pl.BlockSpec(memory_space=pltpu.SMEM), wide, wide, fixed(tokens, state), fixed(tokens, state), fixed(*ld.shape)],
        out_specs=[wide, *[fixed(count // 2, SUB, 2 * state)] * 2, wide, wide, fixed(tokens, LANES)],
        out_shape=[
            pltpu.HBM((tokens, width), F32),
            pltpu.HBM((count // 2, SUB, 2 * state), F32),
            pltpu.HBM((count // 2, SUB, 2 * state), F32),
            pltpu.HBM((tokens, width), BF16),
            pltpu.HBM((tokens, width), BF16),
            pltpu.HBM((tokens, LANES), BF16),
        ],
        scratch_shapes=[
            pltpu.VMEM((tokens, LANES), BF16),
            pltpu.VMEM((tokens, LANES), BF16),
            pltpu.VMEM((tokens, LANES), BF16),
            pltpu.VMEM((2 * count, LANES), BF16),
            pltpu.VMEM((count, SUB, SUB + state), BF16),
            pltpu.VMEM((count, state, SUB), BF16),
            pltpu.VMEM((count, state, SUB), BF16),
            pltpu.VMEM((tokens, WIDE), BF16),
            pltpu.VMEM((tokens, WIDE), BF16),
            pltpu.VMEM((count, SUB + state, SUB + state), F32),
            pltpu.VMEM((count, state, WIDE), F32),
            pltpu.VMEM((count, state, WIDE), F32),
            pltpu.VMEM((count, state, WIDE), BF16),
            pltpu.VMEM((count, state, WIDE), BF16),
        ],
        compiler_params=params(60),
        cost_estimate=pl.CostEstimate(flops=10**10, bytes_accessed=26 * 10**6, transcendentals=0),
        name="local",
    )(place, in_hbm(x), in_hbm(g), w, r, ld)


def meet(kernel, place, x1, g1, states, keep):
    tokens, width = x1.shape
    both = 2 * LANES
    return pl.pallas_call(
        kernel,
        in_specs=[pl.BlockSpec(memory_space=pltpu.SMEM)] + [HERE] * 3,
        out_specs=[HERE] * (1 + keep),
        out_shape=[
            jax.ShapeDtypeStruct((tokens // SUB // 2, SUB, both), F32),
            jax.ShapeDtypeStruct((both, width), BF16),
        ][: 1 + keep],
        compiler_params=params(16),
        cost_estimate=pl.CostEstimate(flops=10**9, bytes_accessed=4 * 10**6, transcendentals=0),
        name="meet_other" if keep else "meet_mine",
    )(place, x1, g1, states)


def finish(gi, own, w, fx, heads):
    tokens, width = gi.shape
    steps = width // WIDE

    def kernel(*refs):
        finish_kernel(*refs, heads=heads)

    return pl.pallas_call(
        kernel,
        in_specs=[HERE] * 4,
        out_specs=pl.BlockSpec(memory_space=pltpu.HBM),
        out_shape=jax.ShapeDtypeStruct((tokens, width), BF16),
        scratch_shapes=[pltpu.VMEM((steps, tokens, WIDE), BF16), pltpu.SemaphoreType.DMA((steps,))],
        compiler_params=params(16),
        cost_estimate=pl.CostEstimate(flops=2 * 10**9, bytes_accessed=13 * 10**6, transcendentals=0),
        name="finish",
    )(gi, own, w, fx)


def over_cores(other):
    ranks = lax.axis_size("head")
    return lax.ppermute(other, "head", [(i, i ^ 1) for i in range(ranks)])


def over_chips(terms):
    ranks = lax.axis_size("head")
    total = [terms[0]]
    for d in sorted(range(1, terms.shape[0]), key=lambda d: -min(d, terms.shape[0] - d)):
        total.append(lax.ppermute(terms[d], "head", [(i, (i + 2 * d) % ranks) for i in range(ranks)]))
    return total


def body(scaled_input, out_grad, write_proj, read_proj, log_decay):
    heads = log_decay.shape[0]
    state = write_proj.shape[1]
    rank = lax.axis_index("head")
    place = jnp.stack([rank // 2, rank % 2]).astype(jnp.int32)
    every = lax.all_to_all(
        summarise(scaled_input, out_grad, write_proj, read_proj, log_decay), "seq", 0, 0, tiled=True
    )
    gi, other, mine, x1, g1, fx = local_gradients(
        place, scaled_input, out_grad, write_proj, read_proj, log_decay
    )
    local = mine + over_cores(other)
    every, place, local, gi, x1, g1, fx = lax.optimization_barrier((every, place, local, gi, x1, g1, fx))
    own = lax.all_to_all(scan_shards(every), "seq", 0, 0, tiled=True)
    other, states = meet(meet_other_kernel, place, x1, g1, own, True)
    arrived = over_cores(other)
    (mine,) = meet(meet_mine_kernel, place, x1, g1, states, False)
    shared = over_chips(mine + arrived + local)
    grad_input = finish(gi, own, write_proj, fx, heads)
    grad_write = sum(part[:, :state] for part in shared).astype(BF16)
    grad_read = sum(part[:, state:] for part in shared).astype(BF16)
    return grad_input, grad_write, grad_read


def solution(mesh):
    return jax.shard_map(
        body,
        mesh=mesh,
        in_specs=(
            P("seq", "head"),
            P("seq", "head"),
            P("seq", None),
            P("seq", None),
            P("head", "seq"),
        ),
        out_specs=(P("seq", "head"), P(("seq", "head"), None), P(("seq", "head"), None)),
        check_vma=False,
    )
```

```python
import jax
import jax.numpy as jnp
from jax import lax
from jax.experimental import pallas as pl
from jax.experimental.pallas import tpu as pltpu
from jax.sharding import PartitionSpec as P

SUB = 128
LANES = 128
WIDE = 512
FIRST = 1024
MIDDLE = SUB // 2 - 1
F32 = jnp.float32
BF16 = jnp.bfloat16


def dot(a, b, dims=((1,), (0,))):
    return lax.dot_general(a, b, (dims, ((), ())), preferred_element_type=F32)


def running_sums(decays):
    rows = lax.broadcasted_iota(jnp.int32, (SUB, SUB), 0)
    columns = lax.broadcasted_iota(jnp.int32, (SUB, SUB), 1)
    lower = jnp.where(rows >= columns, 1.0, 0.0).astype(BF16)
    first = decays.astype(BF16)
    left = decays - first.astype(F32)
    second = left.astype(BF16)
    third = (left - second.astype(F32)).astype(BF16)
    sums = []
    for start in range(0, decays.shape[1], SUB):
        tok = slice(start, start + SUB)
        a, b, c = (dot(lower, term[:, tok], ((1,), (1,))) for term in (first, second, third))
        sums.append(a + (b + c))
    return sums


def two_terms(values, heads):
    lane = lax.broadcasted_iota(jnp.int32, values.shape, 1)
    high = values.astype(BF16).astype(F32)
    kept = jnp.where(lane < heads, high, jnp.where(lane < 2 * heads, values - high, 0.0))
    return kept.astype(BF16)


def spread_matrix(heads, head_size, wide, step):
    row = lax.broadcasted_iota(jnp.int32, (LANES, wide), 0)
    column = lax.broadcasted_iota(jnp.int32, (LANES, wide), 1)
    same = lax.rem(row, heads) == (step * wide + column) // head_size
    return jnp.where(same, 1.0, 0.0).astype(BF16)


def summary_kernel(x_hbm, g_hbm, w_hbm, r_hbm, ld_hbm, out_hbm, fx, fg, ends, wt, rt, xb, gb, w_ref, r_ref, ld_ref, out_ref, sems):
    heads, tokens = ld_ref.shape
    steps, _, wide = xb.shape
    head_size = wide * steps // heads
    state = w_ref.shape[1]
    pairs = wide // LANES

    def load(source, target, step, sem):
        columns = pl.ds(pl.multiple_of(step * wide, wide), wide)
        return pltpu.make_async_copy(source.at[:, columns], target.at[step], sems.at[sem])

    def save(step):
        slots = pl.ds(step * pairs, pairs)
        return pltpu.make_async_copy(out_ref.at[slots], out_hbm.at[slots], sems.at[2 * steps + step])

    small = [
        pltpu.make_async_copy(source, target, sems.at[3 * steps + n])
        for n, (source, target) in enumerate(((ld_hbm, ld_ref), (w_hbm, w_ref), (r_hbm, r_ref)))
    ]
    for copy in small:
        copy.start()
    for step in range(steps):
        load(x_hbm, xb, step, step).start()
        load(g_hbm, gb, step, steps + step).start()

    small[0].wait()
    sums = running_sums(jnp.concatenate([ld_ref[...]] * (LANES // heads), axis=0))
    before = jnp.zeros((1, LANES), F32)
    for k in range(len(sums)):
        sums[k] = sums[k] + before
        before = sums[k][SUB - 1 :]
    for k in range(len(sums)):
        tok = slice(k * SUB, (k + 1) * SUB)
        fx[tok] = two_terms(jnp.exp(before - sums[k]), heads)
        fg[tok] = two_terms(jnp.exp(sums[k]), heads)
    ends[...] = two_terms(jnp.exp(jnp.broadcast_to(before, ends.shape)), heads)
    small[1].wait()
    small[2].wait()
    for start in range(0, tokens, SUB):
        tok = slice(start, start + SUB)
        wt[:, tok] = w_ref[tok].T
        rt[:, tok] = r_ref[tok].T

    for step in range(steps):
        spread = spread_matrix(heads, head_size, wide, step)
        load(x_hbm, xb, step, step).wait()
        written = dot(wt[...], (xb[step].astype(F32) * dot(fx[...], spread)).astype(BF16))
        load(g_hbm, gb, step, steps + step).wait()
        collected = dot(rt[...], (gb[step].astype(F32) * dot(fg[...], spread)).astype(BF16))
        decay = dot(ends[...], spread)[:8]
        for pair in range(pairs):
            lanes = slice(pair * LANES, (pair + 1) * LANES)
            out_ref[step * pairs + pair, :state] = written[:, lanes]
            out_ref[step * pairs + pair, state : 2 * state] = collected[:, lanes]
            out_ref[step * pairs + pair, 2 * state :] = decay[:, lanes]
        save(step).start()
    for step in range(steps):
        save(step).wait()


def scan_kernel(in_ref, out_ref):
    shards = in_ref.shape[0]
    state = out_ref.shape[1] // 2
    carried = jnp.zeros((state, LANES), F32)
    for shard in range(shards):
        out_ref[shard, :state] = carried
        carried = in_ref[shard, 2 * state : 2 * state + 1] * carried + in_ref[shard, :state]
    carried = jnp.zeros((state, LANES), F32)
    for shard in reversed(range(shards)):
        out_ref[shard, state:] = carried
        carried = in_ref[shard, 2 * state : 2 * state + 1] * carried + in_ref[shard, state : 2 * state]


def block_of(place_ref, slot, chips, core):
    return 2 * lax.rem(place_ref[0] + slot, chips) + core


def local_kernel(
    place_ref, x_ref, g_ref, w_ref, r_ref, ld_ref, gi_ref, other_ref, mine_ref, x1_ref, g1_ref, fx, fa, fb, fg, between, pw, wt, rt, xs, gs, acc, wrote, took, into_s, back_s
):
    heads, tokens = ld_ref.shape
    wide = x_ref.shape[1]
    head_size = wide * pl.num_programs(0) // heads
    count, state, _ = wt.shape
    step = pl.program_id(0)
    rows = lax.broadcasted_iota(jnp.int32, (SUB, SUB), 0)
    columns = lax.broadcasted_iota(jnp.int32, (SUB, SUB), 1)
    upper = columns >= rows

    @pl.when(step == 0)
    def _():
        sums = running_sums(jnp.concatenate([ld_ref[...]] * (LANES // heads), axis=0))
        before = jnp.zeros((1, LANES), F32)
        middles = []
        afters = []
        for k in range(count):
            tok = slice(k * SUB, (k + 1) * SUB)
            middle = sums[k][MIDDLE : MIDDLE + 1]
            fa[tok] = two_terms(jnp.exp(middle - sums[k]), heads)
            fb[tok] = two_terms(jnp.exp(sums[k] - middle), heads)
            middles.append(middle)
            afters.append(sums[k][SUB - 1 :] - middle)
            sums[k] = sums[k] + before
            before = sums[k][SUB - 1 :]
            write, read = w_ref[tok], r_ref[tok]
            pairs = jnp.where(upper, dot(write, read, ((1,), (1,))), 0.0).astype(BF16)
            pw[k] = jnp.concatenate([pairs, write], axis=1)
            wt[k] = write.T
            rt[k] = read.T
        into = [middles[0]] + [middles[k] + afters[k - 1] for k in range(1, count)]
        back = [afters[k] + middles[k + 1] for k in range(count - 1)] + [afters[count - 1]]
        between[...] = two_terms(jnp.exp(jnp.concatenate(into + back, axis=0)), heads)
        for k in range(count):
            tok = slice(k * SUB, (k + 1) * SUB)
            fx[tok] = two_terms(jnp.exp(before - sums[k]), heads)
            fg[tok] = two_terms(jnp.exp(sums[k]), heads)
        acc[...] = jnp.zeros_like(acc)

    spread = spread_matrix(heads, head_size, wide, step)
    factor = dot(between[...], spread)
    x1_ref[...] = (x_ref[...].astype(F32) * dot(fx[...], spread)).astype(BF16)
    g1_ref[...] = (g_ref[...].astype(F32) * dot(fg[...], spread)).astype(BF16)
    xs[...] = (x_ref[...].astype(F32) * dot(fa[...], spread)).astype(BF16)
    gs[...] = (g_ref[...].astype(F32) * dot(fb[...], spread)).astype(BF16)
    for k in range(count):
        tok = slice(k * SUB, (k + 1) * SUB)
        took[k] = dot(rt[k], gs[tok])
        wrote[k] = dot(wt[k], xs[tok])

    back = jnp.zeros((state, wide), F32)
    for k in reversed(range(count)):
        back_s[k] = back.astype(BF16)
        if k:
            back = factor[count + k - 1 : count + k] * (back + took[k])
    into = jnp.zeros((state, wide), F32)
    for k in range(count):
        into_s[k] = into.astype(BF16)
        if k + 1 < count:
            into = factor[k + 1 : k + 2] * (into + wrote[k])

    for k in range(count):
        tok = slice(k * SUB, (k + 1) * SUB)
        right = jnp.concatenate([gs[tok], back_s[k]], axis=0)
        left = jnp.concatenate([xs[tok], into_s[k]], axis=0)
        gi_ref[tok] = dot(fa[tok], spread) * dot(pw[k], right)
        acc[k] += dot(left, right, ((1,), (1,)))

    @pl.when(step == pl.num_programs(0) - 1)
    def _():
        for out_ref, core in ((other_ref, 1 - place_ref[1]), (mine_ref, place_ref[1])):
            for slot in range(count // 2):
                k = block_of(place_ref, slot, count // 2, core)
                tok = pl.ds(pl.multiple_of(k * SUB, SUB), SUB)
                weights = jnp.where(upper, acc[k, :SUB, :SUB], 0.0)
                high = weights.astype(BF16)
                rest = (weights - high.astype(F32)).astype(BF16)
                to_write = dot(high, r_ref[tok]) + dot(rest, r_ref[tok])
                to_read = dot(wt[k], high) + dot(wt[k], rest)
                out_ref[slot, :, :state] = to_write + acc[k, :SUB, SUB:]
                out_ref[slot, :, state:] = (to_read + acc[k, SUB:, :SUB]).T


def meet_half(place_ref, away, x1_ref, g1_ref, states, out_ref):
    state = states.shape[0] // 2
    chips = out_ref.shape[0]
    core = 1 - place_ref[1] if away else place_ref[1]
    for slot in range(chips):
        tok = pl.ds(pl.multiple_of(block_of(place_ref, slot, chips, core) * SUB, SUB), SUB)
        out_ref[slot, :, :state] = dot(x1_ref[tok], states[state:], ((1,), (1,)))
        out_ref[slot, :, state:] = dot(g1_ref[tok], states[:state], ((1,), (1,)))


def meet_other_kernel(place_ref, x1_ref, g1_ref, st_ref, out_ref, states):
    for p in range(st_ref.shape[0]):
        states[:, p * LANES : (p + 1) * LANES] = st_ref[p].astype(BF16)
    meet_half(place_ref, True, x1_ref, g1_ref, states, out_ref)


def meet_mine_kernel(place_ref, x1_ref, g1_ref, states, out_ref):
    meet_half(place_ref, False, x1_ref, g1_ref, states, out_ref)


def finish_kernel(gi_ref, st_ref, w_ref, fx, out_hbm, out, sems, *, heads):
    tokens, width = gi_ref.shape
    head_size = width // heads
    state = w_ref.shape[1]
    steps, _, wide = out.shape

    def store(step):
        return pltpu.make_async_copy(out.at[step], out_hbm.at[:, pl.ds(step * wide, wide)], sems.at[step])

    for step in range(steps):
        lanes = slice(step * wide, (step + 1) * wide)
        spread = spread_matrix(heads, head_size, wide, step)
        pairs = range(step * (wide // LANES), (step + 1) * (wide // LANES))
        leaving = jnp.concatenate([st_ref[p, state:].astype(BF16) for p in pairs], axis=1)
        for start in range(0, tokens, WIDE):
            tok = slice(start, start + WIDE)
            out[step, tok] = (gi_ref[tok, lanes] + dot(fx[tok], spread) * dot(w_ref[tok], leaving)).astype(BF16)
        store(step).start()
    for step in range(steps):
        store(step).wait()


def params(mib):
    return pltpu.CompilerParams(vmem_limit_bytes=mib * 2**20)


def in_hbm(array):
    return pltpu.with_memory_space_constraint(array, pltpu.HBM)


HERE = pl.BlockSpec(memory_space=pltpu.VMEM)


def fixed(*shape):
    return pl.BlockSpec(shape, lambda i: (0,) * len(shape))


def summarise(x, g, w, r, ld):
    tokens, width = x.shape
    state = w.shape[1]
    steps = width // FIRST
    there = pl.BlockSpec(memory_space=pltpu.HBM)
    payload = (width // LANES, 2 * state + 8, LANES)
    return pl.pallas_call(
        summary_kernel,
        in_specs=[there] * 5,
        out_specs=there,
        out_shape=jax.ShapeDtypeStruct(payload, F32),
        scratch_shapes=[
            pltpu.VMEM((tokens, LANES), BF16),
            pltpu.VMEM((tokens, LANES), BF16),
            pltpu.VMEM((16, LANES), BF16),
            pltpu.VMEM((state, tokens), BF16),
            pltpu.VMEM((state, tokens), BF16),
            pltpu.VMEM((steps, tokens, FIRST), BF16),
            pltpu.VMEM((steps, tokens, FIRST), BF16),
            pltpu.VMEM((tokens, state), BF16),
            pltpu.VMEM((tokens, state), BF16),
            pltpu.VMEM(ld.shape, F32),
            pltpu.VMEM(payload, F32),
            pltpu.SemaphoreType.DMA((3 * steps + 3,)),
        ],
        compiler_params=params(60),
        name="summary",
    )(x, g, w, r, ld)


def scan_shards(every):
    return pl.pallas_call(
        scan_kernel,
        in_specs=[HERE],
        out_specs=HERE,
        out_shape=jax.ShapeDtypeStruct((every.shape[0], every.shape[1] - 8, LANES), F32),
        compiler_params=params(16),
        name="scan",
    )(every)


def local_gradients(place, x, g, w, r, ld):
    tokens, width = x.shape
    state = w.shape[1]
    count = tokens // SUB
    wide = pl.BlockSpec((tokens, WIDE), lambda i: (0, i))
    return pl.pallas_call(
        local_kernel,
        grid=(width // WIDE,),
        in_specs=[pl.BlockSpec(memory_space=pltpu.SMEM), wide, wide, fixed(tokens, state), fixed(tokens, state), fixed(*ld.shape)],
        out_specs=[wide, *[fixed(count // 2, SUB, 2 * state)] * 2, wide, wide, fixed(tokens, LANES)],
        out_shape=[
            pltpu.HBM((tokens, width), F32),
            pltpu.HBM((count // 2, SUB, 2 * state), F32),
            pltpu.HBM((count // 2, SUB, 2 * state), F32),
            pltpu.HBM((tokens, width), BF16),
            pltpu.HBM((tokens, width), BF16),
            pltpu.HBM((tokens, LANES), BF16),
        ],
        scratch_shapes=[
            pltpu.VMEM((tokens, LANES), BF16),
            pltpu.VMEM((tokens, LANES), BF16),
            pltpu.VMEM((tokens, LANES), BF16),
            pltpu.VMEM((2 * count, LANES), BF16),
            pltpu.VMEM((count, SUB, SUB + state), BF16),
            pltpu.VMEM((count, state, SUB), BF16),
            pltpu.VMEM((count, state, SUB), BF16),
            pltpu.VMEM((tokens, WIDE), BF16),
            pltpu.VMEM((tokens, WIDE), BF16),
            pltpu.VMEM((count, SUB + state, SUB + state), F32),
            pltpu.VMEM((count, state, WIDE), F32),
            pltpu.VMEM((count, state, WIDE), F32),
            pltpu.VMEM((count, state, WIDE), BF16),
            pltpu.VMEM((count, state, WIDE), BF16),
        ],
        compiler_params=params(60),
        cost_estimate=pl.CostEstimate(flops=10**10, bytes_accessed=26 * 10**6, transcendentals=0),
        name="local",
    )(place, in_hbm(x), in_hbm(g), w, r, ld)


def meet(kernel, place, x1, g1, states, keep):
    tokens, width = x1.shape
    both = 2 * LANES
    return pl.pallas_call(
        kernel,
        in_specs=[pl.BlockSpec(memory_space=pltpu.SMEM)] + [HERE] * 3,
        out_specs=[HERE] * (1 + keep),
        out_shape=[
            jax.ShapeDtypeStruct((tokens // SUB // 2, SUB, both), F32),
            jax.ShapeDtypeStruct((both, width), BF16),
        ][: 1 + keep],
        compiler_params=params(16),
        cost_estimate=pl.CostEstimate(flops=10**9, bytes_accessed=4 * 10**6, transcendentals=0),
        name="meet_other" if keep else "meet_mine",
    )(place, x1, g1, states)


def finish(gi, own, w, fx, heads):
    tokens, width = gi.shape
    steps = width // WIDE

    def kernel(*refs):
        finish_kernel(*refs, heads=heads)

    return pl.pallas_call(
        kernel,
        in_specs=[HERE] * 4,
        out_specs=pl.BlockSpec(memory_space=pltpu.HBM),
        out_shape=jax.ShapeDtypeStruct((tokens, width), BF16),
        scratch_shapes=[pltpu.VMEM((steps, tokens, WIDE), BF16), pltpu.SemaphoreType.DMA((steps,))],
        compiler_params=params(16),
        cost_estimate=pl.CostEstimate(flops=2 * 10**9, bytes_accessed=13 * 10**6, transcendentals=0),
        name="finish",
    )(gi, own, w, fx)


def over_cores(other):
    ranks = lax.axis_size("head")
    return lax.ppermute(other, "head", [(i, i ^ 1) for i in range(ranks)])


def over_chips(terms):
    ranks = lax.axis_size("head")
    total = [terms[0]]
    for d in sorted(range(1, terms.shape[0]), key=lambda d: -min(d, terms.shape[0] - d)):
        total.append(lax.ppermute(terms[d], "head", [(i, (i + 2 * d) % ranks) for i in range(ranks)]))
    return total


def body(scaled_input, out_grad, write_proj, read_proj, log_decay):
    heads = log_decay.shape[0]
    state = write_proj.shape[1]
    rank = lax.axis_index("head")
    place = jnp.stack([rank // 2, rank % 2]).astype(jnp.int32)
    every = lax.all_to_all(
        summarise(scaled_input, out_grad, write_proj, read_proj, log_decay), "seq", 0, 0, tiled=True
    )
    gi, other, mine, x1, g1, fx = local_gradients(
        place, scaled_input, out_grad, write_proj, read_proj, log_decay
    )
    local = mine + over_cores(other)
    every, place, local, gi, x1, g1, fx = lax.optimization_barrier((every, place, local, gi, x1, g1, fx))
    own = lax.all_to_all(scan_shards(every), "seq", 0, 0, tiled=True)
    other, states = meet(meet_other_kernel, place, x1, g1, own, True)
    arrived = over_cores(other)
    (mine,) = meet(meet_mine_kernel, place, x1, g1, states, False)
    shared = over_chips(mine + arrived + local)
    grad_input = finish(gi, own, write_proj, fx, heads)
    grad_write = sum(part[:, :state] for part in shared).astype(BF16)
    grad_read = sum(part[:, state:] for part in shared).astype(BF16)
    return grad_input, grad_write, grad_read


def solution(mesh):
    return jax.shard_map(
        body,
        mesh=mesh,
        in_specs=(
            P("seq", "head"),
            P("seq", "head"),
            P("seq", None),
            P("seq", None),
            P("head", "seq"),
        ),
        out_specs=(P("seq", "head"), P(("seq", "head"), None), P(("seq", "head"), None)),
        check_vma=False,
    )
```
